32 devices in a mesh: gx: 4 (over y, core), gy: 8 (over z, x).
Axes of the slice: x: 2, y: 2, z: 4, core: 2. Of those that a mesh axis runs over, the one named last changes fastest.
Arguments:
- log_perm: float32 [32, 256, 128], P('gx', 'gy'), may hold values from -4 to 4
- perturb: float32 [32, 256, 128], P('gx', 'gy'), may hold values from -6 to 6
- storage: float32 [32, 256, 128], P('gx', 'gy'), may hold values from 0.03 to 1
- base_press: float32 [2, 32, 256, 128], P(None, 'gx', 'gy'), may hold values from -6 to 6
- well_rows: float32 [1024, 512], P(('gx', 'gy')), may hold values from 0.002 to 0.02
- well_cells: int32 [1024], P(('gx', 'gy')), may hold values from 0 to 32767
- well_counts: int32 [1024], P(('gx', 'gy')), may hold values from 1 to 512, as said below
- well_owner: int32 [1024, 1], P(('gx', 'gy')), may hold values from 0 to 31; in each aligned block of 32 rows (0 to 31, 32 to 63, ...) at most 2 rows name the same one
- well_start: int32 [1024], P(('gx', 'gy')), may hold values from 0 to 1
Outputs:
- hess_action: float32 [32, 256, 128], P('gx', 'gy')
- final_change: float32 [32, 256, 128], P('gx', 'gy')
The draws below stay inside these ranges and needn't reach their ends.
Inputs may be any that keep to these rules, and one draw needn't show every extreme that they name: `well_owner`: names the device, counted as gx index times 8 plus gy index, whose tile holds the well; among the wells listed on one device no owner appears more than 2 times, and in every draw some device names some owner exactly 2 times. `well_cells`: index x * 32 * 128 + y * 128 + z of the well's cell within its owner's tile. `well_counts`: every draw has a well with all 512 samples and one with a single sample.
All inputs are finite; a program needn't handle non-finite values.
Results may differ from the reference program's by a relative error of at most 0.0001.
Values sent between devices are 32-bit elements; how exact they have to be, the bound alone decides.
No kernel may reach another device: no remote copies, remote signals or barrier semaphores. Data moves between devices by JAX's collectives and lax.ppermute only.
A program may use at most 128 MiB of HBM per device.

```python
import math
import jax
import jax.numpy as jnp
import numpy as np

CX = 8
CY = 32
NZ = 128
TSTEPS = 2
VCYCLES = 2
SWEEPS = 2
CSWEEPS = 4
SAMPLES = 512
CAP = 2
WELLS_DEV = 32
WELLS = 1024
NX = 32
NY = 256
N_GY = 8
DEVICES = 32


def draw_well_counts(key, part):
    counts = jax.random.randint(key, (WELLS,), 1, SAMPLES + 1, dtype=jnp.int32)
    counts = counts.at[0].set(SAMPLES)
    return counts.at[1].set(1)


def touch_ends(drawn, key, low, largest):
    index_at = [jax.random.randint(jax.random.fold_in(key, axis), (), 0, length) for axis, length in enumerate(drawn.shape)]
    longest = drawn.shape.index(max(drawn.shape))
    next_to = index_at[:longest] + [(index_at[longest] + 1) % drawn.shape[longest]] + index_at[longest + 1:]
    return drawn.at[tuple(index_at)].set(low).at[tuple(next_to)].set(largest)


def block_scale(own_key, dims, split, smallest, top_value):
    def one(position, shards_of):
        draws = jax.random.uniform(jax.random.fold_in(jax.random.fold_in(own_key, 6), position), (shards_of,), jnp.float32, smallest / len(split), top_value / len(split))
        return jnp.repeat(jnp.exp(draws), dims[position] // shards_of).reshape((-1,) + (1,) * (len(dims) - position - 1))

    factor_of = one(*split[0])
    for cut in split[1:]:
        factor_of = factor_of * one(*cut)
    return factor_of


def deal_out(key, own, number, rows, amount, top, reach, slope):
    sequence = jax.random.permutation(key, amount)
    crowded, common = load_shares(amount, rows * top, reach, slope, True), load_shares(amount, rows * top, reach, slope, False)
    places = jnp.arange(amount)

    def named(sizes, rotation):
        used = int((sizes > 0).sum())
        fixed = max(1, used // 4)
        moved = fixed + (places - fixed + rotation * (used - fixed)) % max(1, amount - fixed)
        return jnp.zeros((amount,), jnp.int32).at[sequence[jnp.where(places < fixed, places, moved)]].set(jnp.asarray(sizes, jnp.int32))

    sizes = jnp.where(number % 4 == 0, named(crowded, number // 4), named(common, number - number // 4 - 1))
    mixed = jax.random.permutation(jax.random.fold_in(own, 3), amount)
    giver, taker = mixed[0:amount // 2 * 2:2], mixed[1:amount // 2 * 2:2]
    room = jnp.minimum(sizes[giver] - 1, reach - sizes[taker]) // 2
    room = jnp.where((giver == sequence[0]) | (taker == sequence[0]) | (sizes[taker] == 0), 0, jnp.maximum(room, 0))
    moved = jax.random.randint(jax.random.fold_in(own, 4), (amount // 2,), 0, 1 << 20) % (room + 1)
    sizes = sizes.at[giver].add(-moved).at[taker].add(moved)
    items = jnp.searchsorted(jnp.cumsum(sizes), jnp.arange(rows * top), side="right").astype(jnp.int32)
    table = items.reshape(top, rows).T
    table = table[jax.random.permutation(jax.random.fold_in(own, 1), rows)]
    rotation = jax.random.randint(jax.random.fold_in(own, 2), (rows, 1), 0, top)
    return jnp.take_along_axis(table, (jnp.arange(top)[None, :] + rotation) % top, axis=1)


def load_shares(number_of, total, most, lean, full):
    weights = [(1 << 20) // math.isqrt(grade ** lean) + 1 for grade in range(1, number_of + 1)]
    largest = most if full else min(most, max(-(-total // number_of), total * weights[0] // sum(weights)))
    least = 1 if total - largest >= number_of - 1 else 0
    holding, surplus = [largest] + [least] * (number_of - 1), total - largest - least * (number_of - 1)
    while surplus > 0:
        candidates = [i for i in range(1, number_of) if holding[i] < largest] or [i for i in range(1, number_of) if holding[i] < most]
        mass, remaining = sum([weights[i] for i in candidates]), surplus
        for i in candidates:
            addition = min(most - holding[i], max(1, remaining * weights[i] // mass), surplus)
            holding[i] = holding[i] + addition
            surplus = surplus - addition
    return np.array(holding)


def centred(stream_key, extent, deviation, reach, split=(), kind=jnp.bfloat16):
    factor_of = block_scale(stream_key, extent, split, -0.22, 0.18) if split else 1.0
    result = jax.random.normal(stream_key, extent, jnp.float32) * deviation * factor_of
    return jnp.minimum(jnp.maximum(result, -reach), reach).astype(kind)


def setup_inputs(seed: int = 0) -> dict:
    arg_keys = jax.random.split(jax.random.key(seed), 10)
    log_perm = centred(arg_keys[0], (NX, NY, NZ), 1.0, 4.0, ((0, 4), (1, 8)), jnp.float32)
    perturb = centred(arg_keys[1], (NX, NY, NZ), 1.0, 6.0, ((0, 4), (1, 8)), jnp.float32)
    storage = jnp.clip(jnp.exp(math.log(1.0) - 3.506558 * jax.random.uniform(arg_keys[2], (NX, NY, NZ), jnp.float32) ** block_scale(arg_keys[2], (NX, NY, NZ), ((0, 4), (1, 8)), -0.2, 0.2)), 0.03, 1.0)
    base_press = centred(arg_keys[3], (TSTEPS, NX, NY, NZ), 1.0, 6.0, ((1, 4), (2, 8)), jnp.float32)
    well_rows = jnp.clip(jnp.exp(math.log(0.02) - 2.30258502 * jax.random.uniform(arg_keys[4], (WELLS, SAMPLES), jnp.float32) ** block_scale(arg_keys[4], (WELLS, SAMPLES), ((0, 32),), -0.2, 0.2)), 0.002, 0.02)
    well_cells = touch_ends(jax.random.randint(arg_keys[5], (WELLS,), 0, CX * CY * NZ), jax.random.fold_in(arg_keys[5], 1), 0, (CX * CY * NZ) - 1).astype(jnp.int32)
    well_counts = draw_well_counts(jax.random.fold_in(arg_keys[9], 71), 0)
    well_owner_keys = jax.random.split(jax.random.fold_in(arg_keys[7], 1), WELLS // WELLS_DEV)
    well_owner_turns = jax.random.permutation(jax.random.fold_in(arg_keys[7], 3), WELLS // WELLS_DEV)
    well_owner = jax.vmap(lambda own, number: deal_out(jax.random.fold_in(arg_keys[7], 2), own, number, WELLS_DEV, DEVICES, 1, CAP, 0))(well_owner_keys, well_owner_turns).reshape((WELLS, 1))
    well_start = touch_ends(jax.random.randint(arg_keys[8], (WELLS,), 0, TSTEPS), jax.random.fold_in(arg_keys[8], 1), 0, TSTEPS - 1).astype(jnp.int32)
    return {"log_perm": log_perm, "perturb": perturb, "storage": storage, "base_press": base_press, "well_rows": well_rows, "well_cells": well_cells, "well_counts": well_counts, "well_owner": well_owner, "well_start": well_start}


OMEGA = 0.8


def lower_pad(values):
    return jnp.pad(values, ((0, 0), (0, 0), (0, 1)))


def upper_pad(values):
    return jnp.pad(values, ((0, 0), (0, 0), (1, 0)))


def zero_rim(values):
    return jnp.pad(values, ((0, 0), (1, 1), (1, 1), (0, 0)))


def coarsen(values):
    size_x, size_y, size_z = values.shape
    return values.reshape(size_x // 2, 2, size_y // 2, 2, size_z // 2, 2).mean(axis=(1, 3, 5))


def prolong(values):
    return jnp.repeat(jnp.repeat(jnp.repeat(values, 2, 0), 2, 1), 2, 2)


def coefficients(log_pad, storage_level, factor):
    center = log_pad[1:-1, 1:-1]
    along_x = factor * jnp.exp(0.5 * (log_pad[:-1, 1:-1] + log_pad[1:, 1:-1]))
    along_y = factor * jnp.exp(0.5 * (log_pad[1:-1, :-1] + log_pad[1:-1, 1:]))
    along_z = factor * jnp.exp(0.5 * (center[:, :, :-1] + center[:, :, 1:]))
    diagonal = storage_level + along_x[1:] + along_x[:-1] + along_y[:, 1:] + along_y[:, :-1]
    diagonal = diagonal + lower_pad(along_z) + upper_pad(along_z)
    return along_x, along_y, along_z, diagonal


def apply_operator(value_pad, coeffs):
    along_x, along_y, along_z, diagonal = coeffs
    center = value_pad[1:-1, 1:-1]
    beside = along_x[1:] * value_pad[2:, 1:-1] + along_x[:-1] * value_pad[:-2, 1:-1]
    beside = beside + along_y[:, 1:] * value_pad[1:-1, 2:] + along_y[:, :-1] * value_pad[1:-1, :-2]
    beside = beside + lower_pad(along_z * center[:, :, 1:]) + upper_pad(along_z * center[:, :, :-1])
    return diagonal * center - beside


def perturbed(pressure_pad, change_pad, coeffs):
    along_x, along_y, along_z, diagonal = coeffs
    pressure = pressure_pad[1:-1, 1:-1]
    change = change_pad[1:-1, 1:-1]
    summed = along_x[1:] * 0.5 * (change + change_pad[2:, 1:-1]) * (pressure - pressure_pad[2:, 1:-1])
    summed = summed + along_x[:-1] * 0.5 * (change + change_pad[:-2, 1:-1]) * (pressure - pressure_pad[:-2, 1:-1])
    summed = summed + along_y[:, 1:] * 0.5 * (change + change_pad[1:-1, 2:]) * (pressure - pressure_pad[1:-1, 2:])
    summed = summed + along_y[:, :-1] * 0.5 * (change + change_pad[1:-1, :-2]) * (pressure - pressure_pad[1:-1, :-2])
    vertical = along_z * 0.5 * (change[:, :, :-1] + change[:, :, 1:]) * (pressure[:, :, :-1] - pressure[:, :, 1:])
    return summed + lower_pad(vertical) - upper_pad(vertical)


def curvature(pressure_pad, adjoint_pad, coeffs):
    along_x, along_y, along_z, diagonal = coeffs
    pressure = pressure_pad[1:-1, 1:-1]
    adjoint = adjoint_pad[1:-1, 1:-1]
    summed = 0.5 * along_x[1:] * (pressure - pressure_pad[2:, 1:-1]) * (adjoint - adjoint_pad[2:, 1:-1])
    summed = summed + 0.5 * along_x[:-1] * (pressure - pressure_pad[:-2, 1:-1]) * (adjoint - adjoint_pad[:-2, 1:-1])
    summed = summed + 0.5 * along_y[:, 1:] * (pressure - pressure_pad[1:-1, 2:]) * (adjoint - adjoint_pad[1:-1, 2:])
    summed = summed + 0.5 * along_y[:, :-1] * (pressure - pressure_pad[1:-1, :-2]) * (adjoint - adjoint_pad[1:-1, :-2])
    vertical = 0.5 * along_z * (pressure[:, :, :-1] - pressure[:, :, 1:]) * (adjoint[:, :, :-1] - adjoint[:, :, 1:])
    return summed + lower_pad(vertical) + upper_pad(vertical)


def jacobi_sweep(iterate, right_side, coeffs, padder):
    if iterate is None:
        return OMEGA * right_side / coeffs[3]
    padded = padder(iterate[None])[0]
    return iterate + OMEGA * (right_side - apply_operator(padded, coeffs)) / coeffs[3]


def vcycle(iterate, right_side, fine_coeffs, middle_coeffs, fine_pad, middle_pad, coarse_solve):
    current = iterate
    for sweep_index in range(SWEEPS):
        current = jacobi_sweep(current, right_side, fine_coeffs, fine_pad)
    residual = right_side - apply_operator(fine_pad(current[None])[0], fine_coeffs)
    middle_side = coarsen(residual)
    middle = None
    for sweep_index in range(SWEEPS):
        middle = jacobi_sweep(middle, middle_side, middle_coeffs, middle_pad)
    middle_res = middle_side - apply_operator(middle_pad(middle[None])[0], middle_coeffs)
    middle = middle + prolong(coarse_solve(coarsen(middle_res)))
    for sweep_index in range(SWEEPS):
        middle = jacobi_sweep(middle, middle_side, middle_coeffs, middle_pad)
    current = current + prolong(middle)
    for sweep_index in range(SWEEPS):
        current = jacobi_sweep(current, right_side, fine_coeffs, fine_pad)
    return current


def multigrid_solve(right_side, fine_coeffs, middle_coeffs, fine_pad, middle_pad, coarse_solve):
    current = None
    for cycle_index in range(VCYCLES):
        current = vcycle(current, right_side, fine_coeffs, middle_coeffs, fine_pad, middle_pad, coarse_solve)
    return current


def well_weights(records, counts, starts):
    sample_pos = jnp.arange(SAMPLES, dtype=jnp.int32)
    counted = jnp.where(sample_pos[None, :] < counts[:, None], records, 0.0)
    per_step = counted.reshape(records.shape[0], TSTEPS, SAMPLES // TSTEPS).sum(axis=2)
    step_pos = jnp.arange(TSTEPS, dtype=jnp.int32)
    return jnp.where(step_pos[None, :] >= starts[:, None], per_step, 0.0)


def reference(log_perm, perturb, storage, base_press, well_rows, well_cells, well_counts, well_owner, well_start):
    padded = zero_rim(jnp.concatenate([log_perm[None], perturb[None], base_press], axis=0))
    fine_coeffs = coefficients(padded[0], storage, 1.0)
    middle_log = coarsen(log_perm)
    middle_store = coarsen(storage)
    middle_coeffs = coefficients(zero_rim(middle_log[None])[0], middle_store, 0.25)
    coarse_coeffs = coefficients(zero_rim(coarsen(middle_log)[None])[0], coarsen(middle_store), 0.0625)

    def coarse_solve(right_side):
        iterate = None
        for sweep_index in range(CSWEEPS):
            iterate = jacobi_sweep(iterate, right_side, coarse_coeffs, zero_rim)
        return iterate

    def solve_field(right_side):
        return multigrid_solve(right_side, fine_coeffs, middle_coeffs, zero_rim, zero_rim, coarse_solve)

    weights = well_weights(well_rows, well_counts, well_start)
    owner_ids = well_owner[:, 0]
    row_tile = owner_ids // N_GY
    col_tile = owner_ids % N_GY
    local_x = well_cells // (CY * NZ)
    local_y = (well_cells // NZ) % CY
    local_z = well_cells % NZ
    flat_index = ((row_tile * CX + local_x) * NY + col_tile * CY + local_y) * NZ + local_z
    source = jnp.zeros((TSTEPS, NX * NY * NZ), jnp.float32).at[:, flat_index].add(weights.T)
    source = source.reshape(TSTEPS, NX, NY, NZ)

    previous = jnp.zeros(log_perm.shape, jnp.float32)
    changes = []
    for step_index in range(TSTEPS):
        right_side = storage * previous - perturbed(padded[2 + step_index], padded[1], fine_coeffs)
        previous = solve_field(right_side)
        changes.append(previous)
    adjoint_next = jnp.zeros(log_perm.shape, jnp.float32)
    adjoints = [None] * TSTEPS
    for step_index in range(TSTEPS - 1, -1, -1):
        right_side = storage * adjoint_next + source[step_index] * changes[step_index]
        adjoint_next = solve_field(right_side)
        adjoints[step_index] = adjoint_next
    adjoint_pad = zero_rim(jnp.stack(adjoints))
    hessian = jnp.zeros(log_perm.shape, jnp.float32)
    for step_index in range(TSTEPS):
        hessian = hessian - curvature(padded[2 + step_index], adjoint_pad[step_index], fine_coeffs)
    return hessian, changes[-1]
```

```python
import functools

import jax
import jax.numpy as jnp
from jax import lax
from jax.experimental import pallas as pl
from jax.experimental.pallas import tpu as pltpu
from jax.sharding import PartitionSpec as P

OMEGA = 0.8
KEEP = 0.2
VMEM_BYTES = 56 * 2**20

FR, MR, CR = 56, 64, 40
F_OWN, M_OWN = 12, 24
HALO_B, HALO_X = 6, 4
ROWS = 32


def ds(start, size):
    return pl.ds(start, size)


def lanes(shape):
    return lax.broadcasted_iota(jnp.int32, shape, 1)


def loop(count, body, unroll):
    if unroll >= count:
        for index in range(count):
            body(index)
        return

    def step(index, carry):
        body(index)
        return carry

    lax.fori_loop(0, count, step, 0, unroll=unroll)


def neighbours(src, kx, ky, kz, x, start, size, shift):
    rows = ds(start, size)
    center = src[x + 1, rows, :]
    total = kx[x, rows, :] * src[x, rows, :] + kx[x + 1, rows, :] * src[x + 2, rows, :]
    total = total + ky[x, rows, :] * src[x + 1, ds(start + 1, size), :]
    total = total + ky[x, ds(start - 1, size), :] * src[x + 1, ds(start - 1, size), :]
    face = kz[x, rows, :]
    total = total + face * pltpu.roll(center, 128 - shift, 1) + pltpu.roll(face * center, shift, 1)
    return center, total


def sweep(src, dst, coeffs, b, start, size, count, shift, unroll):
    kx, ky, kz, w = coeffs
    rows = ds(start, size)

    def body(x):
        center, total = neighbours(src, kx, ky, kz, x, start, size, shift)
        dst[x + 1, rows, :] = KEEP * center + w[x, rows, :] * (b[x, rows, :] + total)

    loop(count, body, unroll)


def scaled(dst, w, b, start, size, count, unroll):
    rows = ds(start, size)

    def body(x):
        dst[x + 1, rows, :] = w[x, rows, :] * b[x, rows, :]

    loop(count, body, unroll)


def zero_ends(buf, count):
    buf[0] = jnp.zeros(buf.shape[1:], jnp.float32)
    buf[count + 1] = jnp.zeros(buf.shape[1:], jnp.float32)


def seam(buf, count, start, size, fill):
    rows = ds(start, size)
    odd = lanes((size, 128)) % 2 == 1
    buf[0, rows, :] = jnp.where(odd, pltpu.roll(buf[count, rows, :], 1, 1), fill)
    buf[count + 1, rows, :] = jnp.where(odd, fill, pltpu.roll(buf[1, rows, :], 127, 1))


def packed_sweep(src, dst, coeffs, b, start, size, count, shift, unroll):
    sweep(src, dst, coeffs, b, start, size, count, shift, unroll)
    seam(dst, count, start, size, 0.0)


def halve_packed(src, tmp, dst, count):
    for i in range(count // 2):
        tmp[i, ds(8, 48), :] = src[2 * i, ds(8, 48), :] + src[2 * i + 1, ds(8, 48), :]
    low = lanes((24, 128)) % 4 < 2
    for i in range(count // 2):
        both = tmp[i, pl.ds(8, 24, stride=2), :] + tmp[i, pl.ds(9, 24, stride=2), :]
        both = both + jnp.where(low, pltpu.roll(both, 126, 1), pltpu.roll(both, 2, 1))
        dst[i, ds(8, 24), :] = both * 0.125


def middle_solve(own, below, above, mid, coarse, bufs, nx):
    m_b, m_a, m_c, m_res, m_tmp, c_b, c_a, c_c = bufs
    mkx, mky, mkz, mw, mdiag = mid
    count = nx // 4
    for i in range(count):
        m_b[i, ds(8, 16), :] = below(i)
        m_b[i, ds(24, 16), :] = own(i)
        m_b[i, ds(40, 16), :] = above(i)
    scaled(m_c, mw, m_b, 8, 48, count, count)
    seam(m_c, count, 8, 48, 0.0)
    packed_sweep(m_c, m_a, (mkx, mky, mkz, mw), m_b, 8, 48, count, 2, count)
    for i in range(count):
        center, total = neighbours(m_a, mkx, mky, mkz, i, 8, 48, 2)
        m_res[i, ds(8, 48), :] = m_b[i, ds(8, 48), :] + total - mdiag[i, ds(8, 48), :] * center
    halve_packed(m_res, m_tmp, c_b, count)
    half = count // 2
    scaled(c_a, coarse[3], c_b, 8, 24, half, half)
    seam(c_a, half, 8, 24, 0.0)
    packed_sweep(c_a, c_c, coarse, c_b, 8, 24, half, 4, half)
    packed_sweep(c_c, c_a, coarse, c_b, 8, 24, half, 4, half)
    packed_sweep(c_a, c_c, coarse, c_b, 8, 24, half, 4, half)
    for i in range(half):
        value = c_c[i + 1, ds(12, 16), :]
        m_tmp[i, pl.ds(16, 16, stride=2), :] = value
        m_tmp[i, pl.ds(17, 16, stride=2), :] = value
        for j in range(2):
            x = 2 * i + j + 1
            m_a[x, ds(16, 32), :] = m_a[x, ds(16, 32), :] + m_tmp[i, ds(16, 32), :]
    seam(m_a, count, 16, 32, 0.0)
    packed_sweep(m_a, m_c, (mkx, mky, mkz, mw), m_b, 16, 32, count, 2, count)
    packed_sweep(m_c, m_a, (mkx, mky, mkz, mw), m_b, 16, 32, count, 2, count)


def add_correction(x_buf, m_a, f_tmp, nx, unroll):
    count = nx // 4
    odd = lanes((24, 128)) % 2 == 1
    for i in range(count):
        value = m_a[i + 1, ds(20, 24), :]
        first = jnp.where(odd, pltpu.roll(value, 1, 1), value)
        second = jnp.where(odd, value, pltpu.roll(value, 127, 1))
        for part, slab in ((first, i), (second, i + count)):
            f_tmp[slab, pl.ds(4, 24, stride=2), :] = part
            f_tmp[slab, pl.ds(5, 24, stride=2), :] = part

    def body(i):
        value = f_tmp[i, ds(4, 48), :]
        for j in range(2):
            x = 2 * i + j + 1
            x_buf[x, ds(4, 48), :] = x_buf[x, ds(4, 48), :] + value

    loop(nx // 2, body, unroll)


def restricted(x_buf, coeffs, diag, b, f_tmp, outs, nx, unroll):
    kx, ky, kz, w = coeffs
    count = nx // 4

    def body(i):
        both = None
        for j in range(2):
            x = 2 * i + j
            center, total = neighbours(x_buf, kx, ky, kz, x, F_OWN, ROWS, 1)
            part = b[x, ds(F_OWN, ROWS), :] + total - diag[x] * center
            both = part if both is None else both + part
        f_tmp[i, ds(0, ROWS), :] = both

    loop(nx // 2, body, unroll)
    odd = lanes((16, 128)) % 2 == 1
    for i in range(count):
        first = f_tmp[i, pl.ds(0, 16, stride=2), :] + f_tmp[i, pl.ds(1, 16, stride=2), :]
        second = f_tmp[i + count, pl.ds(0, 16, stride=2), :] + f_tmp[i + count, pl.ds(1, 16, stride=2), :]
        value = 0.125 * jnp.where(
            odd, second + pltpu.roll(second, 1, 1), first + pltpu.roll(first, 127, 1)
        )
        for out in outs:
            out(i, value)


def gather_rhs(b_buf, b_own, below, above, nx):
    for x in range(nx):
        b_buf[x, ds(F_OWN, ROWS), :] = b_own[x]
        b_buf[x, ds(F_OWN - HALO_B, HALO_B), :] = below[ds(x * HALO_B, HALO_B), :]
        b_buf[x, ds(F_OWN + ROWS, HALO_B), :] = above[ds(x * HALO_B, HALO_B), :]


def message_writers(ups, downs, b1_own, base):
    def write(i, value):
        ups[ds(base + 16 * i, 16), :] = value
        downs[ds(base + 16 * i, 16), :] = value
        b1_own[i] = value

    return [write]


def message_part(ref, base):
    return lambda i: ref[ds(base + 16 * i, 16), :]


def begin_solve(b_buf, x_a, x_b, coeffs, diag, f_tmp, b_own, b1_own, up, down, nx, unroll):
    scaled(x_a, coeffs[3], b_buf, 8, 40, nx, unroll)
    sweep(x_a, x_b, coeffs, b_buf, 8, 40, nx, 1, unroll)
    base = nx * HALO_B
    restricted(x_b, coeffs, diag, b_buf, f_tmp, message_writers(up, down, b1_own, base), nx, unroll)
    for x in range(nx):
        b_own[x] = b_buf[x, ds(F_OWN, ROWS), :]
        up[ds(x * HALO_B, HALO_B), :] = b_buf[x, ds(F_OWN + ROWS - HALO_B, HALO_B), :]
        down[ds(x * HALO_B, HALO_B), :] = b_buf[x, ds(F_OWN, HALO_B), :]


def first_kernel(log, sto, per, bp, own, up, down, tmp):
    odd = lanes((16, 128)) % 2 == 1
    fields = (log, sto, per, bp.at[0], bp.at[1])
    for f, ref in enumerate(fields):
        for x in range(8):
            own[ds(f * 256 + x * 32, 32), :] = ref[x]
    for f in range(2):
        for x in range(8):
            up[ds(f * 64 + x * 8, 8), :] = fields[f][x, ds(24, 8), :]
            down[ds(f * 64 + x * 8, 8), :] = fields[f][x, ds(0, 8), :]
    for f in range(3):
        for x in range(8):
            up[ds(128 + f * 32 + x * 4, 4), :] = fields[f + 2][x, ds(28, 4), :]
            down[ds(128 + f * 32 + x * 4, 4), :] = fields[f + 2][x, ds(0, 4), :]
    for i in range(4):
        tmp[0, i] = log[2 * i] + log[2 * i + 1]
        tmp[1, i] = sto[2 * i] + sto[2 * i + 1]
    for i in range(4):
        first, second = (
            tmp[f, i, pl.ds(0, 16, stride=2), :] + tmp[f, i, pl.ds(1, 16, stride=2), :] for f in range(2)
        )
        value = 0.125 * jnp.where(
            odd, second + pltpu.roll(second, 1, 1), first + pltpu.roll(first, 127, 1)
        )
        own[ds(1280 + 16 * i, 16), :] = value
        up[ds(224 + 16 * i, 16), :] = value
        down[ds(224 + 16 * i, 16), :] = value


def faces(e, kx, ky, kz, count, size, shift, factor, unroll):
    top = lanes((size, 128)) >= 128 - shift

    def body(x):
        kx[x] = factor * e[x] * e[x + 1]
        center = e[x + 1]
        kz[x] = jnp.where(top, 0.0, factor * center * pltpu.roll(center, 128 - shift, 1))
        ky[x, ds(0, size - 8), :] = factor * e[x + 1, ds(0, size - 8), :] * e[x + 1, ds(1, size - 8), :]
        ky[x, ds(size - 8, 8), :] = jnp.zeros((8, 128), jnp.float32)

    loop(count, body, unroll)
    kx[count] = factor * e[count] * e[count + 1]


def diagonal(sto, kx, ky, kz, x, start, size, shift):
    rows = ds(start, size)
    face = kz[x, rows, :]
    total = sto + kx[x, rows, :] + kx[x + 1, rows, :] + ky[x, rows, :] + ky[x, ds(start - 1, size), :]
    return total + face + pltpu.roll(face, shift, 1)


def inside(size, own_start, own_size, first, last):
    row = lax.broadcasted_iota(jnp.int32, (size, 128), 0)
    return jnp.logical_and(
        jnp.logical_or(row >= own_start, jnp.logical_not(first)),
        jnp.logical_or(row < own_start + own_size, jnp.logical_not(last)),
    )


def second_kernel(nx, n_gy, unroll, *refs):
    tiles = nx // 8
    place = refs[0]
    owns, halos = refs[1 : 1 + tiles], refs[1 + tiles : 1 + 2 * tiles]
    (kx, ky, kz, w, diag, sto_out, d_one, bp_out, mkx, mky, mkz, mw, mdiag, ckx, cky, ckz, cw) = refs[
        1 + 2 * tiles : 18 + 2 * tiles
    ]
    b_own, b1_own, up, down = refs[18 + 2 * tiles : 22 + 2 * tiles]
    e, sto, per, bp0, bp1, x_a, x_b, b_buf, f_tmp, e_mid, s_mid, e_co, s_co, m_tmp, m_tmp2 = refs[22 + 2 * tiles :]
    gx, gy = place[0], place[1]
    first, last = gy == 0, gy == n_gy - 1
    for buf in (e, per, bp0, bp1, x_a, x_b):
        zero_ends(buf, nx)
    half, core = tiles // 2, gx % 2

    def tile_of(index):
        k, other = index % half, index // half
        return ((gx // 2 + half - k) % half) * 2 + (core + other) % 2

    blank = jnp.zeros((4, 128), jnp.float32)
    blank8 = jnp.zeros((8, 128), jnp.float32)
    keep_low = jnp.where(first, 0.0, 1.0)
    keep_high = jnp.where(last, 0.0, 1.0)
    for index in range(tiles):
        own, halo = owns[index], halos[index]
        base = tile_of(index) * 8

        def body(x, own=own, halo=halo, base=base):
            for f, buf in enumerate((e, sto, per, bp0, bp1)):
                slab = base + x + (0 if f == 1 else 1)
                buf[slab, ds(12, 32), :] = own[ds(f * 256 + x * 32, 32), :]
                if f < 2:
                    buf[slab, ds(4, 8), :] = halo[ds(f * 64 + x * 8, 8), :]
                    buf[slab, ds(44, 8), :] = halo[ds(288 + f * 64 + x * 8, 8), :]
                    buf[slab, ds(0, 4), :] = blank
                    buf[slab, ds(52, 4), :] = blank
                else:
                    at = 128 + (f - 2) * 32 + x * 4
                    buf[slab, ds(0, 8), :] = blank8
                    buf[slab, ds(48, 8), :] = blank8
                    buf[slab, ds(8, 4), :] = halo[ds(at, 4), :] * keep_low
                    buf[slab, ds(44, 4), :] = halo[ds(288 + at, 4), :] * keep_high

        for x in range(8):
            body(x)
    fine_inside = inside(FR, F_OWN, ROWS, first, last)

    def exps(x):
        e[x + 1] = jnp.where(fine_inside, jnp.exp(0.5 * e[x + 1]), 1.0)

    loop(nx, exps, unroll)
    e[0] = jnp.ones((FR, 128), jnp.float32)
    e[nx + 1] = jnp.ones((FR, 128), jnp.float32)
    faces(e, kx, ky, kz, nx, FR, 1, 1.0, unroll)
    win_inside = inside(48, F_OWN - 4, ROWS, first, last)

    def diagonals(x):
        value = diagonal(sto[x, ds(4, 48), :], kx, ky, kz, x, 4, 48, 1)
        w[x, ds(4, 48), :] = jnp.where(win_inside, OMEGA / value, 0.0)
        w[x, ds(0, 4), :] = blank
        w[x, ds(52, 4), :] = blank
        diag[x] = value[8:40]
        sto_out[x] = sto[x, ds(8, 40), :]

    loop(nx, diagonals, unroll)

    def changes(x):
        rows, plus, minus = ds(8, 40), ds(9, 40), ds(7, 40)
        kl, kr, kp, km, face = kx[x, rows, :], kx[x + 1, rows, :], ky[x, rows, :], ky[x, minus, :], kz[x, rows, :]
        c = per[x + 1, rows, :]
        weights = (
            kl * 0.5 * (c + per[x, rows, :]),
            kr * 0.5 * (c + per[x + 2, rows, :]),
            km * 0.5 * (c + per[x + 1, minus, :]),
            kp * 0.5 * (c + per[x + 1, plus, :]),
            face * 0.5 * (c + pltpu.roll(c, 127, 1)),
        )
        for t, bp in enumerate((bp0, bp1)):
            p = bp[x + 1, rows, :]
            total = weights[0] * (p - bp[x, rows, :]) + weights[1] * (p - bp[x + 2, rows, :])
            total = total + weights[2] * (p - bp[x + 1, minus, :]) + weights[3] * (p - bp[x + 1, plus, :])
            flux = weights[4] * (p - pltpu.roll(p, 127, 1))
            total = total + flux - pltpu.roll(flux, 1, 1)
            if t == 0:
                b_buf[x, rows, :] = -total
            else:
                d_one[x] = total

    loop(nx, changes, unroll)
    for x in range(10):
        bp_out[0, x] = bp0[gx * 8 + x]
        bp_out[1, x] = bp1[gx * 8 + x]

    count = nx // 4
    odd = lanes((16, 128)) % 2 == 1
    for index in range(tiles):
        own, halo = owns[index], halos[index]
        tile = tile_of(index)
        upper = tile >= half
        base = jnp.where(upper, tile - half, tile) * 4
        mask = odd == upper
        for i in range(4):
            for start, ref, at in ((8, halo, 224 + 16 * i), (24, own, 1280 + 16 * i), (40, halo, 512 + 16 * i)):
                value = ref[ds(at, 16), :]
                left, right = pltpu.roll(value, 127, 1), pltpu.roll(value, 1, 1)
                log_part, sto_part = jnp.where(odd, right, value), jnp.where(odd, value, left)
                rows = ds(start, 16)
                e_mid[base + i + 1, rows, :] = jnp.where(mask, log_part, e_mid[base + i + 1, rows, :])
                s_mid[base + i, rows, :] = jnp.where(mask, sto_part, s_mid[base + i, rows, :])
    for i in range(count):
        m_tmp2[i] = e_mid[i + 1]
    halve_packed(m_tmp2, m_tmp, e_co.at[pl.ds(1, count // 2)], count)
    halve_packed(s_mid, m_tmp, s_co, count)
    levels = (
        (e_mid, s_mid, mkx, mky, mkz, mw, mdiag, count, MR, M_OWN, 16, 2, 0.25),
        (e_co, s_co, ckx, cky, ckz, cw, None, count // 2, CR, 16, 8, 4, 0.0625),
    )
    for e_l, s_l, kx_l, ky_l, kz_l, w_l, diag_l, number, size, own_start, own_size, shift, factor in levels:
        ok = inside(size, own_start, own_size, first, last)
        row = lax.broadcasted_iota(jnp.int32, (size, 128), 0)
        ok = jnp.logical_and(ok, jnp.logical_and(row >= 8, row < size - 8))
        for i in range(number):
            e_l[i + 1] = jnp.where(ok, jnp.exp(0.5 * e_l[i + 1]), 1.0)
        seam(e_l, number, 0, size, 1.0)
        faces(e_l, kx_l, ky_l, kz_l, number, size, shift, factor, number)
        rows = ds(8, size - 16)
        edge = jnp.zeros((8, 128), jnp.float32)
        for i in range(number):
            value = diagonal(s_l[i, rows, :], kx_l, ky_l, kz_l, i, 8, size - 16, shift)
            w_l[i, rows, :] = jnp.where(ok[8 : size - 8], OMEGA / value, 0.0)
            w_l[i, ds(0, 8), :] = edge
            w_l[i, ds(size - 8, 8), :] = edge
            if diag_l is not None:
                diag_l[i, rows, :] = value
                diag_l[i, ds(0, 8), :] = edge
                diag_l[i, ds(size - 8, 8), :] = edge
    begin_solve(b_buf, x_a, x_b, (kx, ky, kz, w), diag, f_tmp, b_own, b1_own, up, down, nx, unroll)


def middle_kernel(nx, unroll, *refs):
    (kx, ky, kz, w, diag, mkx, mky, mkz, mw, mdiag, ckx, cky, ckz, cw) = refs[:14]
    b_own, b1_own, below, above, x_own, b1_out, up, down = refs[14:22]
    x_a, x_b, b_buf, f_tmp = refs[22:26]
    bufs = refs[26:]
    coeffs = (kx, ky, kz, w)
    zero_ends(x_a, nx)
    zero_ends(x_b, nx)
    base = nx * HALO_B
    middle_solve(
        lambda i: b1_own[i],
        message_part(below, base),
        message_part(above, base),
        (mkx, mky, mkz, mw, mdiag),
        (ckx, cky, ckz, cw),
        bufs,
        nx,
    )
    gather_rhs(b_buf, b_own, below, above, nx)
    scaled(x_a, w, b_buf, 4, 48, nx, unroll)
    sweep(x_a, x_b, coeffs, b_buf, 4, 48, nx, 1, unroll)
    add_correction(x_b, bufs[1], f_tmp, nx, unroll)
    sweep(x_b, x_a, coeffs, b_buf, 8, 40, nx, 1, unroll)
    sweep(x_a, x_b, coeffs, b_buf, 8, 40, nx, 1, unroll)
    sweep(x_b, x_a, coeffs, b_buf, 8, 40, nx, 1, unroll)
    sweep(x_a, x_b, coeffs, b_buf, 8, 40, nx, 1, unroll)
    base = nx * HALO_X
    restricted(x_b, coeffs, diag, b_buf, f_tmp, message_writers(up, down, b1_out, base), nx, unroll)
    for x in range(nx):
        x_own[x] = x_b[x + 1, ds(F_OWN, ROWS), :]
        up[ds(x * HALO_X, HALO_X), :] = x_b[x + 1, ds(F_OWN + ROWS - HALO_X, HALO_X), :]
        down[ds(x * HALO_X, HALO_X), :] = x_b[x + 1, ds(F_OWN, HALO_X), :]


def end_kernel(nx, n_gy, unroll, kind, *refs):
    place = refs[0]
    (kx, ky, kz, w, diag, mkx, mky, mkz, mw, mdiag, ckx, cky, ckz, cw) = refs[1:15]
    b_in, below_b, above_b, x_own, b1_in, below, above = refs[15:22]
    extra = {1: 2, 2: 1, 3: 3, 4: 2}[kind]
    extras, rest = refs[22 : 22 + extra], refs[22 + extra :]
    outs = {1: 5, 2: 5, 3: 5, 4: 1}[kind]
    outs, scratch = rest[:outs], rest[outs:]
    x_a, x_b, b_buf, f_tmp = scratch[:4]
    bufs = scratch[4:]
    coeffs = (kx, ky, kz, w)
    gx, gy = place[0], place[1]
    keep_low = jnp.where(gy == 0, 0.0, 1.0)
    keep_high = jnp.where(gy == n_gy - 1, 0.0, 1.0)
    zero_ends(x_a, nx)
    zero_ends(x_b, nx)
    base = nx * HALO_X
    middle_solve(
        lambda i: b1_in[i],
        message_part(below, base),
        message_part(above, base),
        (mkx, mky, mkz, mw, mdiag),
        (ckx, cky, ckz, cw),
        bufs,
        nx,
    )
    gather_rhs(b_buf, b_in, below_b, above_b, nx)
    for x in range(nx):
        x_a[x + 1, ds(F_OWN, ROWS), :] = x_own[x]
        x_a[x + 1, ds(F_OWN - HALO_X, HALO_X), :] = below[ds(x * HALO_X, HALO_X), :] * keep_low
        x_a[x + 1, ds(F_OWN + ROWS, HALO_X), :] = above[ds(x * HALO_X, HALO_X), :] * keep_high
    add_correction(x_a, bufs[1], f_tmp, nx, unroll)
    sweep(x_a, x_b, coeffs, b_buf, 8, 40, nx, 1, unroll)
    sweep(x_b, x_a, coeffs, b_buf, 8, 40, nx, 1, unroll)
    rows = ds(8, 40)
    if kind < 4:
        b_own, b1_own, up, down, kept = outs

        def body(x):
            value = x_a[x + 1, rows, :]
            if kind == 1:
                sto, d_one = extras
                b_buf[x, rows, :] = sto[x] * value - d_one[x]
            elif kind == 2:
                b_buf[x, rows, :] = extras[0][x] * value
            else:
                sto, source, change = extras
                b_buf[x, rows, :] = sto[x] * value + source[x] * change[x]
            if kind == 1:
                kept[x] = value
            elif kind == 3:
                kept[x + 1] = value

        loop(nx, body, unroll)
        if kind == 2:
            for x in range(8):
                kept[x] = x_a[gx * 8 + x + 1, ds(F_OWN, ROWS), :]
        if kind == 3:
            zero_ends(kept, nx)
        begin_solve(b_buf, x_a, x_b, coeffs, diag, f_tmp, b_own, b1_own, up, down, nx, unroll)
    else:
        lam_two, bp = extras
        own, plus, minus = ds(F_OWN, ROWS), ds(F_OWN + 1, ROWS), ds(F_OWN - 1, ROWS)
        for x in range(8):
            at = gx * 8 + x
            kl, kr, kp, km, face = kx[at, own, :], kx[at + 1, own, :], ky[at, own, :], ky[at, minus, :], kz[at, own, :]
            total = None
            for t, (lam, shift) in enumerate(((x_a, 0), (lam_two, 8))):
                low, mid, high = (ds(F_OWN - shift + step, ROWS) for step in (-1, 0, 1))
                p, v = bp[t, x + 1, own, :], lam[at + 1, mid, :]
                part = kl * (p - bp[t, x, own, :]) * (v - lam[at, mid, :])
                part = part + kr * (p - bp[t, x + 2, own, :]) * (v - lam[at + 2, mid, :])
                part = part + km * (p - bp[t, x + 1, minus, :]) * (v - lam[at + 1, low, :])
                part = part + kp * (p - bp[t, x + 1, plus, :]) * (v - lam[at + 1, high, :])
                flux = face * (p - pltpu.roll(p, 127, 1)) * (v - pltpu.roll(v, 127, 1))
                part = part + flux + pltpu.roll(flux, 1, 1)
                total = part if total is None else total + part
            outs[0][x] = -0.5 * total


def call(body, outs, scratch, args, scalars):
    f32 = jnp.float32
    vmem = pl.BlockSpec(memory_space=pltpu.VMEM)
    smem = pl.BlockSpec(memory_space=pltpu.SMEM)
    return pl.pallas_call(
        body,
        out_shape=[jax.ShapeDtypeStruct(s, f32) for s in outs],
        in_specs=[smem] * scalars + [vmem] * (len(args) - scalars),
        out_specs=[vmem] * len(outs),
        scratch_shapes=[pltpu.VMEM(s, f32) for s in scratch],
        compiler_params=pltpu.CompilerParams(vmem_limit_bytes=VMEM_BYTES),
    )(*args)


def cycle(count, step):
    return [(i, (i + step) % count) for i in range(count)]


def gathered(array, tiles):
    half = tiles // 2
    same = [array]
    for k in range(1, half):
        perm = [(2 * a + c, 2 * ((a + k) % half) + c) for a in range(half) for c in range(2)]
        same.append(lax.ppermute(array, "gx", perm))
    swap = [(i, i ^ 1) for i in range(tiles)]
    return same + [lax.ppermute(part, "gx", swap) for part in same]


def well_sources(rows, cells, counts, owners, starts, nx, n_gy):
    listed, samples = rows.shape
    steps = 2
    position = jnp.arange(samples, dtype=jnp.int32)
    counted = jnp.where(position[None, :] < counts[:, None], rows, 0.0)
    per_step = counted.reshape(listed, steps, samples // steps).sum(axis=2)
    weights = jnp.where(jnp.arange(steps, dtype=jnp.int32)[None, :] >= starts[:, None], per_step, 0.0)
    whole = jnp.stack([owners[:, 0], cells], axis=0)
    weights = lax.all_gather(weights.T, ("gx", "gy"), axis=1, tiled=True)
    whole = lax.all_gather(whole, ("gx", "gy"), axis=1, tiled=True)
    owner, cell = whole[0], whole[1]
    x = (owner // n_gy) * 8 + cell // (32 * 128)
    y = (owner % n_gy - lax.axis_index("gy")) * 32 + (cell // 128) % 32 + 4
    spot = jnp.where(jnp.logical_and(y >= 0, y < 40), x * 40 + y, -1)
    z = cell % 128
    total = spot.shape[0]
    chunk = 1024 if total % 1024 == 0 else total

    def part(spot, z, weights):
        left = (spot[None, :] == jnp.arange(nx * 40, dtype=jnp.int32)[:, None]).astype(jnp.float32)
        here = z[:, None] == jnp.arange(128, dtype=jnp.int32)[None, :]
        right = jnp.concatenate([jnp.where(here, weights[t][:, None], 0.0) for t in range(steps)], axis=1)
        return jnp.dot(left, right, precision=lax.Precision.HIGHEST)

    if total == chunk:
        source = part(spot, z, weights)
    else:

        def body(i, acc):
            cut = lambda a: lax.dynamic_slice_in_dim(a, i * chunk, chunk, axis=-1)
            return acc + part(cut(spot), cut(z), cut(weights))

        source = lax.fori_loop(0, total // chunk, body, jnp.zeros((nx * 40, steps * 128), jnp.float32))
    return [source[:, t * 128 : (t + 1) * 128].reshape(nx, 40, 128) for t in range(steps)]


def local(log_perm, perturb, storage, base_press, well_rows, well_cells, well_counts, well_owner, well_start):
    tiles, n_gy = lax.axis_size("gx"), lax.axis_size("gy")
    nx = 8 * tiles
    count, half = nx // 4, nx // 8
    unroll = 8
    up_perm, down_perm = cycle(n_gy, 1), cycle(n_gy, -1)

    def exchange(up, down):
        return lax.ppermute(up, "gy", up_perm), lax.ppermute(down, "gy", down_perm)

    place = jnp.stack([lax.axis_index("gx"), lax.axis_index("gy")]).astype(jnp.int32)
    own, up, down = call(
        first_kernel, [(1344, 128), (288, 128), (288, 128)], [(2, 4, 32, 128)], [log_perm, storage, perturb, base_press], 0
    )
    below, above = exchange(up, down)
    owns = gathered(own, tiles)
    halos = gathered(jnp.concatenate([below, above], axis=0), tiles)

    fine, fine_pad, mid, mid_pad = (nx, FR, 128), (nx + 2, FR, 128), (count, MR, 128), (count + 2, MR, 128)
    coarse, coarse_pad = (half, CR, 128), (half + 2, CR, 128)
    own_shape, window = (nx, ROWS, 128), (nx, 40, 128)
    b1_shape = (count, 16, 128)
    message_b, message_x = (nx * HALO_B + count * 16, 128), (nx * HALO_X + count * 16, 128)
    coeff_shapes = [(nx + 1, FR, 128), fine, fine, fine, own_shape]
    mid_shapes = [(count + 1, MR, 128), mid, mid, mid, mid]
    coarse_shapes = [(half + 1, CR, 128), coarse, coarse, coarse]
    outs = call(
        functools.partial(second_kernel, nx, n_gy, min(unroll, 4)),
        coeff_shapes
        + [window, window, (2, 10, FR, 128)]
        + mid_shapes
        + coarse_shapes
        + [own_shape, b1_shape, message_b, message_b],
        [fine_pad, fine, fine_pad, fine_pad, fine_pad, fine_pad, fine_pad, fine, (nx // 2, FR, 128)]
        + [mid_pad, mid, coarse_pad, coarse, mid, mid],
        [place] + owns + halos,
        1,
    )
    coeffs, (sto, d_one, bp) = outs[:5], outs[5:8]
    coeffs = list(coeffs) + list(outs[8:17])
    begun = outs[17:21]
    sources = well_sources(well_rows, well_cells, well_counts, well_owner, well_start, nx, n_gy)
    scratch = [fine_pad, fine_pad, fine, (nx // 2, FR, 128)]
    scratch += [mid, mid_pad, mid_pad, mid, mid, coarse, coarse_pad, coarse_pad]
    change = None
    for kind in (1, 2, 3, 4):
        b_own, b1_own, up, down = begun
        below_b, above_b = exchange(up, down)
        x_own, b1_mid, up, down = call(
            functools.partial(middle_kernel, nx, unroll),
            [own_shape, b1_shape, message_x, message_x],
            scratch,
            coeffs + [b_own, b1_own, below_b, above_b],
            0,
        )
        below, above = exchange(up, down)
        extras = {1: [sto, d_one], 2: [sources[1]], 3: [sto, sources[0], change], 4: []}[kind]
        begin_shapes = [own_shape, b1_shape, message_b, message_b]
        shapes = {
            1: begin_shapes + [window],
            2: begin_shapes + [(8, ROWS, 128)],
            3: begin_shapes + [(nx + 2, 40, 128)],
            4: [(8, ROWS, 128)],
        }[kind]
        if kind == 4:
            extras = [lam_two, bp]
        outs = call(
            functools.partial(end_kernel, nx, n_gy, unroll, kind),
            shapes,
            scratch,
            [place] + coeffs + [b_own, below_b, above_b, x_own, b1_mid, below, above] + extras,
            1,
        )
        if kind == 1:
            change = outs[4]
        elif kind == 2:
            final_change = outs[4]
        elif kind == 3:
            lam_two = outs[4]
        begun = outs[:4]
    return (outs[0], final_change)


def solution(mesh):
    return jax.shard_map(
        local,
        mesh=mesh,
        in_specs=(
            P("gx", "gy", None),
            P("gx", "gy", None),
            P("gx", "gy", None),
            P(None, "gx", "gy", None),
            P(("gx", "gy"), None),
            P(("gx", "gy")),
            P(("gx", "gy")),
            P(("gx", "gy"), None),
            P(("gx", "gy")),
        ),
        out_specs=(P("gx", "gy", None), P("gx", "gy", None)),
        check_vma=False,
    )
```

```python
import functools

import jax
import jax.numpy as jnp
from jax import lax
from jax.experimental import pallas as pl
from jax.experimental.pallas import tpu as pltpu
from jax.sharding import PartitionSpec as P

OMEGA = 0.8
KEEP = 0.2
VMEM_BYTES = 32 * 2**20
WELLS = 8

FR, MR, CR = 56, 64, 40
F_OWN, M_OWN = 12, 24
HALO_B, SKIP_B, HALO_X, SKIP_X = 4, 2, 3, 1
REACH_B, REACH_X = 14, 12
ROWS = 32


def ds(start, size):
    return pl.ds(start, size)


def lanes(shape):
    return lax.broadcasted_iota(jnp.int32, shape, 1)


def loop(count, body, unroll):
    if unroll >= count:
        for index in range(count):
            body(index)
        return

    def step(index, carry):
        body(index)
        return carry

    lax.fori_loop(0, count, step, 0, unroll=unroll)


def neighbours(src, kx, ky, kz, x, start, size, shift):
    rows = ds(start, size)
    center = src[x + 1, rows, :]
    total = kx[x, rows, :] * src[x, rows, :] + kx[x + 1, rows, :] * src[x + 2, rows, :]
    total = total + ky[x, rows, :] * src[x + 1, ds(start + 1, size), :]
    total = total + ky[x, ds(start - 1, size), :] * src[x + 1, ds(start - 1, size), :]
    face = kz[x, rows, :]
    total = total + face * pltpu.roll(center, 128 - shift, 1) + pltpu.roll(face * center, shift, 1)
    return center, total


def sweep(src, dst, coeffs, b, start, size, count, shift, unroll):
    kx, ky, kz, w = coeffs
    rows = ds(start, size)

    def body(x):
        center, total = neighbours(src, kx, ky, kz, x, start, size, shift)
        dst[x + 1, rows, :] = KEEP * center + w[x, rows, :] * (b[x, rows, :] + total)

    loop(count, body, unroll)


def scaled(dst, w, b, start, size, count, unroll):
    rows = ds(start, size)

    def body(x):
        dst[x + 1, rows, :] = w[x, rows, :] * b[x, rows, :]

    loop(count, body, unroll)


def zero_ends(buf, count):
    buf[0] = jnp.zeros(buf.shape[1:], jnp.float32)
    buf[count + 1] = jnp.zeros(buf.shape[1:], jnp.float32)


def seam(buf, count, start, size, fill):
    rows = ds(start, size)
    odd = lanes((size, 128)) % 2 == 1
    buf[0, rows, :] = jnp.where(odd, pltpu.roll(buf[count, rows, :], 1, 1), fill)
    buf[count + 1, rows, :] = jnp.where(odd, fill, pltpu.roll(buf[1, rows, :], 127, 1))


def packed_sweep(src, dst, coeffs, b, start, size, count, shift, unroll):
    sweep(src, dst, coeffs, b, start, size, count, shift, unroll)
    seam(dst, count, start, size, 0.0)


def halve_packed(src, tmp, dst, count):
    for i in range(count // 2):
        tmp[i, ds(8, 48), :] = src[2 * i, ds(8, 48), :] + src[2 * i + 1, ds(8, 48), :]
    low = lanes((24, 128)) % 4 < 2
    for i in range(count // 2):
        both = tmp[i, pl.ds(8, 24, stride=2), :] + tmp[i, pl.ds(9, 24, stride=2), :]
        both = both + jnp.where(low, pltpu.roll(both, 126, 1), pltpu.roll(both, 2, 1))
        dst[i, ds(8, 24), :] = both * 0.125


def middle_solve(own, below, above, reach, mid, coarse, bufs, nx):
    m_b, m_a, m_c, m_res, m_tmp, c_b, c_a, c_c = bufs
    mkx, mky, mkz, mw, mdiag = mid
    count = nx // 4
    for i in range(count):
        m_b[i, ds(M_OWN - reach, reach), :] = below(i)
        m_b[i, ds(M_OWN, 16), :] = own(i)
        m_b[i, ds(M_OWN + 16, reach), :] = above(i)
    scaled(m_c, mw, m_b, 8, 48, count, count)
    seam(m_c, count, 8, 48, 0.0)
    packed_sweep(m_c, m_a, (mkx, mky, mkz, mw), m_b, 8, 48, count, 2, count)
    for i in range(count):
        center, total = neighbours(m_a, mkx, mky, mkz, i, 8, 48, 2)
        m_res[i, ds(8, 48), :] = m_b[i, ds(8, 48), :] + total - mdiag[i, ds(8, 48), :] * center
    halve_packed(m_res, m_tmp, c_b, count)
    half = count // 2
    scaled(c_a, coarse[3], c_b, 8, 24, half, half)
    seam(c_a, half, 8, 24, 0.0)
    packed_sweep(c_a, c_c, coarse, c_b, 8, 24, half, 4, half)
    packed_sweep(c_c, c_a, coarse, c_b, 8, 24, half, 4, half)
    packed_sweep(c_a, c_c, coarse, c_b, 8, 24, half, 4, half)
    for i in range(half):
        value = c_c[i + 1, ds(12, 16), :]
        m_tmp[i, pl.ds(16, 16, stride=2), :] = value
        m_tmp[i, pl.ds(17, 16, stride=2), :] = value
        for j in range(2):
            x = 2 * i + j + 1
            m_a[x, ds(16, 32), :] = m_a[x, ds(16, 32), :] + m_tmp[i, ds(16, 32), :]
    seam(m_a, count, 16, 32, 0.0)
    packed_sweep(m_a, m_c, (mkx, mky, mkz, mw), m_b, 16, 32, count, 2, count)
    packed_sweep(m_c, m_a, (mkx, mky, mkz, mw), m_b, 16, 32, count, 2, count)


def add_correction(x_buf, m_a, f_tmp, nx, unroll):
    count = nx // 4
    odd = lanes((24, 128)) % 2 == 1
    for i in range(count):
        value = m_a[i + 1, ds(20, 24), :]
        first = jnp.where(odd, pltpu.roll(value, 1, 1), value)
        second = jnp.where(odd, value, pltpu.roll(value, 127, 1))
        for part, slab in ((first, i), (second, i + count)):
            f_tmp[slab, pl.ds(4, 24, stride=2), :] = part
            f_tmp[slab, pl.ds(5, 24, stride=2), :] = part

    def body(i):
        value = f_tmp[i, ds(4, 48), :]
        for j in range(2):
            x = 2 * i + j + 1
            x_buf[x, ds(4, 48), :] = x_buf[x, ds(4, 48), :] + value

    loop(nx // 2, body, unroll)


def restricted(x_buf, coeffs, diag, b, f_tmp, outs, nx, unroll):
    kx, ky, kz, w = coeffs
    count = nx // 4

    def body(i):
        both = None
        for j in range(2):
            x = 2 * i + j
            center, total = neighbours(x_buf, kx, ky, kz, x, F_OWN, ROWS, 1)
            part = b[x, ds(F_OWN, ROWS), :] + total - diag[x] * center
            both = part if both is None else both + part
        f_tmp[i, ds(0, ROWS), :] = both

    loop(nx // 2, body, unroll)
    odd = lanes((16, 128)) % 2 == 1
    for i in range(count):
        first = f_tmp[i, pl.ds(0, 16, stride=2), :] + f_tmp[i, pl.ds(1, 16, stride=2), :]
        second = f_tmp[i + count, pl.ds(0, 16, stride=2), :] + f_tmp[i + count, pl.ds(1, 16, stride=2), :]
        value = 0.125 * jnp.where(
            odd, second + pltpu.roll(second, 1, 1), first + pltpu.roll(first, 127, 1)
        )
        for out in outs:
            out(i, value)


def gather_rows(buf, window, below, above, halo, skip, nx, pad, keep_low=None, keep_high=None):
    low, high = F_OWN - skip - halo, F_OWN + ROWS + skip
    for x in range(nx):
        buf[x + pad, ds(8, 40), :] = window[x]
        under, over = below[ds(x * halo, halo), :], above[ds(x * halo, halo), :]
        buf[x + pad, ds(low, halo), :] = under if keep_low is None else under * keep_low
        buf[x + pad, ds(high, halo), :] = over if keep_high is None else over * keep_high


def send_rows(up, down, buf, halo, skip, nx, pad):
    for x in range(nx):
        up[ds(x * halo, halo), :] = buf[x + pad, ds(F_OWN + ROWS - skip - halo, halo), :]
        down[ds(x * halo, halo), :] = buf[x + pad, ds(F_OWN + skip, halo), :]


def message_writers(ups, downs, b1_own, base, reach):
    def write(i, value):
        ups[ds(base + reach * i, reach), :] = value[16 - reach :]
        downs[ds(base + reach * i, reach), :] = value[:reach]
        b1_own[i] = value

    return [write]


def message_part(ref, base, reach):
    return lambda i: ref[ds(base + reach * i, reach), :]


def begin_solve(b_buf, x_a, x_b, coeffs, diag, f_tmp, b_out, x_out, b1_own, up, down, nx, unroll):
    scaled(x_a, coeffs[3], b_buf, 8, 40, nx, unroll)
    sweep(x_a, x_b, coeffs, b_buf, 8, 40, nx, 1, unroll)
    writers = message_writers(up, down, b1_own, nx * HALO_B, REACH_B)
    restricted(x_b, coeffs, diag, b_buf, f_tmp, writers, nx, unroll)
    for x in range(nx):
        b_out[x] = b_buf[x, ds(8, 40), :]
        x_out[x] = x_b[x + 1, ds(8, 40), :]
    send_rows(up, down, b_buf, HALO_B, SKIP_B, nx, 0)


def listed_wells(rows, counts, cells, owners, starts, masked):
    number, samples = rows.shape
    position = lanes((1, samples))
    lane = lanes((1, 128))
    listed = [jnp.full((1, 128), -1.0, jnp.float32)] + [jnp.zeros((1, 128), jnp.float32)] * 2
    masked[...] = jnp.zeros(masked.shape, jnp.float32)
    for i in range(number):
        masked[ds(i, 1), :] = jnp.where(position < counts[i], rows[ds(i, 1), :], 0.0)
        for j, ref in enumerate((owners, cells, starts)):
            listed[j] = jnp.where(lane == i, ref[i].astype(jnp.float32), listed[j])
    step = lax.broadcasted_iota(jnp.int32, (8, samples), 0)
    taken = jnp.where(lanes((8, samples)) // (samples // 2) == step, 1.0, 0.0)
    sums = lax.dot_general(
        taken, masked[...], (((1,), (1,)), ((), ())), precision=lax.Precision.HIGHEST, preferred_element_type=jnp.float32
    )
    return listed[0], listed[1], jnp.where(listed[2] <= 0.0, sums[0:1], 0.0), sums[1:2]


def first_kernel(use_list, *refs):
    if use_list:
        counts, cells, owners, starts, log, sto, per, bp, rows, own, up, down, tmp, masked = refs
    else:
        log, sto, per, bp, own, up, down, tmp = refs
    for ref, at in ((own, 1344), (up, 288), (down, 288)):
        ref[ds(at, WELLS), :] = jnp.zeros((WELLS, 128), jnp.float32)
    if use_list:
        for j, value in enumerate(listed_wells(rows, counts, cells, owners, starts, masked)):
            for ref, at in ((own, 1344), (up, 288), (down, 288)):
                ref[ds(at + j, 1), :] = value
    odd = lanes((16, 128)) % 2 == 1
    fields = (log, sto, per, bp.at[0], bp.at[1])
    for f, ref in enumerate(fields):
        for x in range(8):
            own[ds(f * 256 + x * 32, 32), :] = ref[x]
    for f in range(2):
        for x in range(8):
            up[ds(f * 64 + x * 8, 8), :] = fields[f][x, ds(24, 8), :]
            down[ds(f * 64 + x * 8, 8), :] = fields[f][x, ds(0, 8), :]
    for f in range(3):
        for x in range(8):
            up[ds(128 + f * 32 + x * 4, 4), :] = fields[f + 2][x, ds(28, 4), :]
            down[ds(128 + f * 32 + x * 4, 4), :] = fields[f + 2][x, ds(0, 4), :]
    for i in range(4):
        tmp[0, i] = log[2 * i] + log[2 * i + 1]
        tmp[1, i] = sto[2 * i] + sto[2 * i + 1]
    for i in range(4):
        first, second = (
            tmp[f, i, pl.ds(0, 16, stride=2), :] + tmp[f, i, pl.ds(1, 16, stride=2), :] for f in range(2)
        )
        value = 0.125 * jnp.where(
            odd, second + pltpu.roll(second, 1, 1), first + pltpu.roll(first, 127, 1)
        )
        own[ds(1280 + 16 * i, 16), :] = value
        up[ds(224 + 16 * i, 16), :] = value
        down[ds(224 + 16 * i, 16), :] = value


def faces(e, kx, ky, kz, count, size, shift, factor, unroll):
    top = lanes((size, 128)) >= 128 - shift

    def body(x):
        kx[x] = factor * e[x] * e[x + 1]
        center = e[x + 1]
        kz[x] = jnp.where(top, 0.0, factor * center * pltpu.roll(center, 128 - shift, 1))
        for start, number in ((0, size - 8), (size - 8, 7)):
            ky[x, ds(start, number), :] = factor * e[x + 1, ds(start, number), :] * e[x + 1, ds(start + 1, number), :]
        ky[x, ds(size - 1, 1), :] = jnp.zeros((1, 128), jnp.float32)

    loop(count, body, unroll)
    kx[count] = factor * e[count] * e[count + 1]


def diagonal(sto, kx, ky, kz, x, start, size, shift):
    rows = ds(start, size)
    face = kz[x, rows, :]
    total = sto + kx[x, rows, :] + kx[x + 1, rows, :] + ky[x, rows, :] + ky[x, ds(start - 1, size), :]
    return total + face + pltpu.roll(face, shift, 1)


def inside(size, own_start, own_size, first, last):
    row = lax.broadcasted_iota(jnp.int32, (size, 128), 0)
    return jnp.logical_and(
        jnp.logical_or(row >= own_start, jnp.logical_not(first)),
        jnp.logical_or(row < own_start + own_size, jnp.logical_not(last)),
    )


def second_kernel(nx, n_gy, unroll, *refs):
    tiles = nx // 8
    place = refs[0]
    owns, halos = refs[1 : 1 + tiles], refs[1 + tiles : 1 + 2 * tiles]
    (kx, ky, kz, w, diag, sto_out, d_one, bp_out, mkx, mky, mkz, mw, mdiag, ckx, cky, ckz, cw) = refs[
        1 + 2 * tiles : 18 + 2 * tiles
    ]
    b_out, x_out, b1_own, up, down, wells = refs[18 + 2 * tiles : 24 + 2 * tiles]
    e, sto, per, bp0, bp1, x_a, x_b, b_buf, f_tmp, e_mid, s_mid, e_co, s_co, m_tmp, m_tmp2 = refs[24 + 2 * tiles :]
    gx, gy = place[0], place[1]
    first, last = gy == 0, gy == n_gy - 1
    for buf in (e, per, bp0, bp1, x_a, x_b):
        zero_ends(buf, nx)
    half, core = tiles // 2, gx % 2

    def tile_of(index):
        k, other = index % half, index // half
        return ((gx // 2 + half - k) % half) * 2 + (core + other) % 2

    blank = jnp.zeros((4, 128), jnp.float32)
    blank8 = jnp.zeros((8, 128), jnp.float32)
    keep_low = jnp.where(first, 0.0, 1.0)
    keep_high = jnp.where(last, 0.0, 1.0)
    for index in range(tiles):
        own, halo = owns[index], halos[index]
        base = tile_of(index) * 8

        def body(x, own=own, halo=halo, base=base):
            for f, buf in enumerate((e, sto, per, bp0, bp1)):
                slab = base + x + (0 if f == 1 else 1)
                buf[slab, ds(12, 32), :] = own[ds(f * 256 + x * 32, 32), :]
                if f < 2:
                    buf[slab, ds(4, 8), :] = halo[ds(f * 64 + x * 8, 8), :]
                    buf[slab, ds(44, 8), :] = halo[ds(296 + f * 64 + x * 8, 8), :]
                    buf[slab, ds(0, 4), :] = blank
                    buf[slab, ds(52, 4), :] = blank
                else:
                    at = 128 + (f - 2) * 32 + x * 4
                    buf[slab, ds(0, 8), :] = blank8
                    buf[slab, ds(48, 8), :] = blank8
                    buf[slab, ds(8, 4), :] = halo[ds(at, 4), :] * keep_low
                    buf[slab, ds(44, 4), :] = halo[ds(296 + at, 4), :] * keep_high

        for x in range(8):
            body(x)
    fine_inside = inside(FR, F_OWN, ROWS, first, last)

    def exps(x):
        e[x + 1] = jnp.where(fine_inside, jnp.exp(0.5 * e[x + 1]), 1.0)

    loop(nx, exps, unroll)
    e[0] = jnp.ones((FR, 128), jnp.float32)
    e[nx + 1] = jnp.ones((FR, 128), jnp.float32)
    faces(e, kx, ky, kz, nx, FR, 1, 1.0, unroll)
    win_inside = inside(48, F_OWN - 4, ROWS, first, last)

    def diagonals(x):
        value = diagonal(sto[x, ds(4, 48), :], kx, ky, kz, x, 4, 48, 1)
        w[x, ds(4, 48), :] = jnp.where(win_inside, OMEGA / value, 0.0)
        w[x, ds(0, 4), :] = blank
        w[x, ds(52, 4), :] = blank
        diag[x] = value[8:40]
        sto_out[x] = sto[x, ds(8, 40), :]

    loop(nx, diagonals, unroll)

    def changes(x):
        rows, plus, minus = ds(8, 40), ds(9, 40), ds(7, 40)
        kl, kr, kp, km, face = kx[x, rows, :], kx[x + 1, rows, :], ky[x, rows, :], ky[x, minus, :], kz[x, rows, :]
        c = per[x + 1, rows, :]
        weights = (
            kl * 0.5 * (c + per[x, rows, :]),
            kr * 0.5 * (c + per[x + 2, rows, :]),
            km * 0.5 * (c + per[x + 1, minus, :]),
            kp * 0.5 * (c + per[x + 1, plus, :]),
            face * 0.5 * (c + pltpu.roll(c, 127, 1)),
        )
        for t, bp in enumerate((bp0, bp1)):
            p = bp[x + 1, rows, :]
            total = weights[0] * (p - bp[x, rows, :]) + weights[1] * (p - bp[x + 2, rows, :])
            total = total + weights[2] * (p - bp[x + 1, minus, :]) + weights[3] * (p - bp[x + 1, plus, :])
            flux = weights[4] * (p - pltpu.roll(p, 127, 1))
            total = total + flux - pltpu.roll(flux, 1, 1)
            if t == 0:
                b_buf[x, rows, :] = -total
            else:
                d_one[x] = total

    loop(nx, changes, unroll)
    for x in range(10):
        bp_out[0, x] = bp0[gx * 8 + x]
        bp_out[1, x] = bp1[gx * 8 + x]

    lane = lanes((WELLS, 128))
    listed = 128 // tiles
    for refs_of, at, out in ((owns, 1344, wells), (halos, 288, up), (halos, 584, down)):
        value = refs_of[0][ds(at, WELLS), :]
        for index in range(1, tiles):
            moved = pltpu.roll(refs_of[index][ds(at, WELLS), :], index * listed, 1)
            value = jnp.where(lane >= index * listed, moved, value)
        out[ds(out.shape[0] - WELLS, WELLS), :] = value

    count = nx // 4
    odd = lanes((16, 128)) % 2 == 1
    for index in range(tiles):
        own, halo = owns[index], halos[index]
        tile = tile_of(index)
        upper = tile >= half
        base = jnp.where(upper, tile - half, tile) * 4
        mask = odd == upper
        for i in range(4):
            for start, ref, at in ((8, halo, 224 + 16 * i), (24, own, 1280 + 16 * i), (40, halo, 520 + 16 * i)):
                value = ref[ds(at, 16), :]
                left, right = pltpu.roll(value, 127, 1), pltpu.roll(value, 1, 1)
                log_part, sto_part = jnp.where(odd, right, value), jnp.where(odd, value, left)
                rows = ds(start, 16)
                e_mid[base + i + 1, rows, :] = jnp.where(mask, log_part, e_mid[base + i + 1, rows, :])
                s_mid[base + i, rows, :] = jnp.where(mask, sto_part, s_mid[base + i, rows, :])
    for i in range(count):
        m_tmp2[i] = e_mid[i + 1]
    halve_packed(m_tmp2, m_tmp, e_co.at[pl.ds(1, count // 2)], count)
    halve_packed(s_mid, m_tmp, s_co, count)
    levels = (
        (e_mid, s_mid, mkx, mky, mkz, mw, mdiag, count, MR, M_OWN, 16, 2, 0.25),
        (e_co, s_co, ckx, cky, ckz, cw, None, count // 2, CR, 16, 8, 4, 0.0625),
    )
    for e_l, s_l, kx_l, ky_l, kz_l, w_l, diag_l, number, size, own_start, own_size, shift, factor in levels:
        ok = inside(size, own_start, own_size, first, last)
        row = lax.broadcasted_iota(jnp.int32, (size, 128), 0)
        ok = jnp.logical_and(ok, jnp.logical_and(row >= 8, row < size - 8))
        for i in range(number):
            e_l[i + 1] = jnp.where(ok, jnp.exp(0.5 * e_l[i + 1]), 1.0)
        seam(e_l, number, 0, size, 1.0)
        faces(e_l, kx_l, ky_l, kz_l, number, size, shift, factor, number)
        rows = ds(8, size - 16)
        edge = jnp.zeros((8, 128), jnp.float32)
        for i in range(number):
            value = diagonal(s_l[i, rows, :], kx_l, ky_l, kz_l, i, 8, size - 16, shift)
            w_l[i, rows, :] = jnp.where(ok[8 : size - 8], OMEGA / value, 0.0)
            w_l[i, ds(0, 8), :] = edge
            w_l[i, ds(size - 8, 8), :] = edge
            if diag_l is not None:
                diag_l[i, rows, :] = value
                diag_l[i, ds(0, 8), :] = edge
                diag_l[i, ds(size - 8, 8), :] = edge
    begin_solve(b_buf, x_a, x_b, (kx, ky, kz, w), diag, f_tmp, b_out, x_out, b1_own, up, down, nx, unroll)


def forward(below, above, up, down):
    up[ds(up.shape[0] - WELLS, WELLS), :] = below[ds(below.shape[0] - WELLS, WELLS), :]
    down[ds(down.shape[0] - WELLS, WELLS), :] = above[ds(above.shape[0] - WELLS, WELLS), :]


def middle_kernel(nx, unroll, *refs):
    b1_own, below, above, mkx, mky, mkz, mw, mdiag, ckx, cky, ckz, cw = refs[:12]
    b_in, x_in, kx, ky, kz, w, diag, x_out, b1_out, up, down = refs[12:23]
    x_a, x_b, b_buf, f_tmp = refs[23:27]
    bufs = refs[27:]
    coeffs = (kx, ky, kz, w)
    zero_ends(x_a, nx)
    zero_ends(x_b, nx)
    base = nx * HALO_B
    forward(below, above, up, down)
    middle_solve(
        lambda i: b1_own[i],
        message_part(below, base, REACH_B),
        message_part(above, base, REACH_B),
        REACH_B,
        (mkx, mky, mkz, mw, mdiag),
        (ckx, cky, ckz, cw),
        bufs,
        nx,
    )
    gather_rows(b_buf, b_in, below, above, HALO_B, SKIP_B, nx, 0)
    for start in (0, 40):
        scaled(x_a, w, b_buf, start, 16, nx, unroll)
    for x in range(nx):
        x_b[x + 1, ds(8, 40), :] = x_in[x]
    for start in (4, 44):
        sweep(x_a, x_b, coeffs, b_buf, start, 8, nx, 1, unroll)
    add_correction(x_b, bufs[1], f_tmp, nx, unroll)
    sweep(x_b, x_a, coeffs, b_buf, 8, 40, nx, 1, unroll)
    sweep(x_a, x_b, coeffs, b_buf, 8, 40, nx, 1, unroll)
    sweep(x_b, x_a, coeffs, b_buf, 8, 40, nx, 1, unroll)
    sweep(x_a, x_b, coeffs, b_buf, 8, 40, nx, 1, unroll)
    base = nx * HALO_X
    restricted(x_b, coeffs, diag, b_buf, f_tmp, message_writers(up, down, b1_out, base, REACH_X), nx, unroll)
    for x in range(nx):
        x_out[x] = x_b[x + 1, ds(8, 40), :]
    send_rows(up, down, x_b, HALO_X, SKIP_X, nx, 1)


def end_kernel(nx, n_gy, unroll, kind, *refs):
    place = refs[0]
    b1_in, below, above, mkx, mky, mkz, mw, mdiag, ckx, cky, ckz, cw = refs[1:13]
    below_b, above_b, b_in, x_in, kx, ky, kz, w, diag = refs[13:22]
    extra = {1: 2, 2: 1, 3: 3, 4: 2}[kind]
    extras, rest = refs[22 : 22 + extra], refs[22 + extra :]
    outs = {1: 6, 2: 6, 3: 6, 4: 1}[kind]
    outs, scratch = rest[:outs], rest[outs:]
    x_a, x_b, b_buf, f_tmp = scratch[:4]
    bufs = scratch[4:]
    coeffs = (kx, ky, kz, w)
    gx, gy = place[0], place[1]
    keep_low = jnp.where(gy == 0, 0.0, 1.0)
    keep_high = jnp.where(gy == n_gy - 1, 0.0, 1.0)
    zero_ends(x_a, nx)
    zero_ends(x_b, nx)
    base = nx * HALO_X
    if kind < 4:
        forward(below, above, outs[3], outs[4])
    middle_solve(
        lambda i: b1_in[i],
        message_part(below, base, REACH_X),
        message_part(above, base, REACH_X),
        REACH_X,
        (mkx, mky, mkz, mw, mdiag),
        (ckx, cky, ckz, cw),
        bufs,
        nx,
    )
    gather_rows(b_buf, b_in, below_b, above_b, HALO_B, SKIP_B, nx, 0)
    gather_rows(x_a, x_in, below, above, HALO_X, SKIP_X, nx, 1, keep_low, keep_high)
    add_correction(x_a, bufs[1], f_tmp, nx, unroll)
    sweep(x_a, x_b, coeffs, b_buf, 8, 40, nx, 1, unroll)
    sweep(x_b, x_a, coeffs, b_buf, 8, 40, nx, 1, unroll)
    rows = ds(8, 40)
    if kind < 4:
        b_out, x_out, b1_own, up, down, kept = outs

        def body(x):
            value = x_a[x + 1, rows, :]
            if kind == 1:
                sto, d_one = extras
                b_buf[x, rows, :] = sto[x] * value - d_one[x]
            elif kind == 2:
                b_buf[x, rows, :] = extras[0][x] * value
            else:
                sto, source, change = extras
                b_buf[x, rows, :] = sto[x] * value + source[x] * change[x]
            if kind == 1:
                kept[x] = value
            elif kind == 3:
                kept[x + 1] = value

        loop(nx, body, unroll)
        if kind == 2:
            for x in range(8):
                kept[x] = x_a[gx * 8 + x + 1, ds(F_OWN, ROWS), :]
        if kind == 3:
            zero_ends(kept, nx)
        begin_solve(b_buf, x_a, x_b, coeffs, diag, f_tmp, b_out, x_out, b1_own, up, down, nx, unroll)
    else:
        lam_two, bp = extras
        own, plus, minus = ds(F_OWN, ROWS), ds(F_OWN + 1, ROWS), ds(F_OWN - 1, ROWS)
        for x in range(8):
            at = gx * 8 + x
            kl, kr, kp, km, face = kx[at, own, :], kx[at + 1, own, :], ky[at, own, :], ky[at, minus, :], kz[at, own, :]
            total = None
            for t, (lam, shift) in enumerate(((x_a, 0), (lam_two, 8))):
                low, mid, high = (ds(F_OWN - shift + step, ROWS) for step in (-1, 0, 1))
                p, v = bp[t, x + 1, own, :], lam[at + 1, mid, :]
                part = kl * (p - bp[t, x, own, :]) * (v - lam[at, mid, :])
                part = part + kr * (p - bp[t, x + 2, own, :]) * (v - lam[at + 2, mid, :])
                part = part + km * (p - bp[t, x + 1, minus, :]) * (v - lam[at + 1, low, :])
                part = part + kp * (p - bp[t, x + 1, plus, :]) * (v - lam[at + 1, high, :])
                flux = face * (p - pltpu.roll(p, 127, 1)) * (v - pltpu.roll(v, 127, 1))
                part = part + flux + pltpu.roll(flux, 1, 1)
                total = part if total is None else total + part
            outs[0][x] = -0.5 * total


def call(body, outs, scratch, args, scalars, limit=VMEM_BYTES):
    f32 = jnp.float32
    staged = [i for i, arg in enumerate(args) if i >= scalars and arg.ndim == 1]
    held_at = len(args) + len(outs)

    def kernel(*refs):
        refs = list(refs)
        if staged:
            semaphores = refs[-1]
            copies = []
            for j, i in enumerate(staged):
                copies.append(pltpu.make_async_copy(refs[i], refs[held_at + j], semaphores.at[j]))
                copies[-1].start()
            for j, i in enumerate(staged):
                copies[j].wait()
                refs[i] = refs[held_at + j]
            refs = refs[:-1]
        body(*refs[:held_at], *refs[held_at + len(staged) :])

    return pl.pallas_call(
        kernel,
        out_shape=[jax.ShapeDtypeStruct(shape, f32) for shape in outs],
        in_specs=[pl.BlockSpec(memory_space=pltpu.SMEM)] * scalars
        + [pl.BlockSpec(memory_space=pltpu.VMEM)] * (len(args) - scalars),
        out_specs=[pl.BlockSpec(memory_space=pltpu.VMEM)] * len(outs),
        scratch_shapes=[pltpu.SMEM(args[i].shape, args[i].dtype) for i in staged]
        + [pltpu.VMEM(shape, f32) for shape in scratch]
        + ([pltpu.SemaphoreType.DMA((len(staged),))] if staged else []),
        compiler_params=pltpu.CompilerParams(vmem_limit_bytes=limit),
    )(*args)


def cycle(count, step):
    return [(i, (i + step) % count) for i in range(count)]


def gathered(array, tiles):
    half = tiles // 2
    same = [array]
    for k in range(1, half):
        perm = [(2 * a + c, 2 * ((a + k) % half) + c) for a in range(half) for c in range(2)]
        same.append(lax.ppermute(array, "gx", perm))
    swap = [(i, i ^ 1) for i in range(tiles)]
    return same + [lax.ppermute(part, "gx", swap) for part in same]


def gathered_wells(rows, cells, counts, owners, starts):
    listed, samples = rows.shape
    position = jnp.arange(samples, dtype=jnp.int32)
    counted = jnp.where(position[None, :] < counts[:, None], rows, 0.0)
    per_step = counted.reshape(listed, 2, samples // 2).sum(axis=2)
    weights = jnp.where(jnp.arange(2, dtype=jnp.int32)[None, :] >= starts[:, None], per_step, 0.0)
    places = jnp.stack([owners, cells], axis=0).astype(jnp.float32)
    return lax.all_gather(jnp.concatenate([places, weights.T], axis=0), ("gx", "gy"), axis=1, tiled=True)


def well_sources(wells, nx, n_gy):
    owner, cell, weights = wells[0].astype(jnp.int32), wells[1].astype(jnp.int32), wells[2:4]
    x = (owner // n_gy) * 8 + cell // (32 * 128)
    y = (owner % n_gy - lax.axis_index("gy")) * 32 + (cell // 128) % 32 + 4
    spot = jnp.where(jnp.logical_and(owner >= 0, jnp.logical_and(y >= 0, y < 40)), x * 40 + y, -1)
    z = cell % 128
    total = spot.shape[0]
    chunk = 1024 if total % 1024 == 0 else total

    def part(spot, z, weights):
        left = (spot[None, :] == jnp.arange(nx * 40, dtype=jnp.int32)[:, None]).astype(jnp.float32)
        here = z[:, None] == jnp.arange(128, dtype=jnp.int32)[None, :]
        right = jnp.concatenate([jnp.where(here, weights[t][:, None], 0.0) for t in range(2)], axis=1)
        return jnp.dot(left, right, precision=lax.Precision.HIGHEST)

    if total == chunk:
        source = part(spot, z, weights)
    else:

        def body(i, acc):
            cut = lambda a: lax.dynamic_slice_in_dim(a, i * chunk, chunk, axis=-1)
            return acc + part(cut(spot), cut(z), cut(weights))

        source = lax.fori_loop(0, total // chunk, body, jnp.zeros((nx * 40, 256), jnp.float32))
    return [source[:, t * 128 : (t + 1) * 128].reshape(nx, 40, 128) for t in range(2)]


def local(log_perm, perturb, storage, base_press, well_rows, well_cells, well_counts, well_owner, well_start):
    tiles, n_gy = lax.axis_size("gx"), lax.axis_size("gy")
    nx = 8 * tiles
    count, half = nx // 4, nx // 8
    unroll = 32
    up_perm, down_perm = cycle(n_gy, 1), cycle(n_gy, -1)

    def exchange(up, down):
        return lax.ppermute(up, "gy", up_perm), lax.ppermute(down, "gy", down_perm)

    place = jnp.stack([lax.axis_index("gx"), lax.axis_index("gy")]).astype(jnp.int32)
    listed, samples = well_rows.shape
    owners = well_owner.reshape(listed)
    use_list = n_gy == 8 and tiles * listed == 128
    own, up, down = call(
        functools.partial(first_kernel, use_list),
        [(1344 + WELLS, 128), (288 + WELLS, 128), (288 + WELLS, 128)],
        [(2, 4, 32, 128)] + ([(128, samples)] if use_list else []),
        ([well_counts, well_cells, owners, well_start] if use_list else [])
        + [log_perm, storage, perturb, base_press]
        + ([well_rows] if use_list else []),
        0,
        60 * 2**20,
    )
    below, above = exchange(up, down)
    owns = gathered(own, tiles)
    halos = gathered(jnp.concatenate([below, above], axis=0), tiles)

    fine, fine_pad, mid, mid_pad = (nx, FR, 128), (nx + 2, FR, 128), (count, MR, 128), (count + 2, MR, 128)
    coarse, coarse_pad = (half, CR, 128), (half + 2, CR, 128)
    own_shape, window = (nx, ROWS, 128), (nx, 40, 128)
    b1_shape = (count, 16, 128)
    message_b = (nx * HALO_B + count * REACH_B + WELLS, 128)
    message_x = (nx * HALO_X + count * REACH_X + WELLS, 128)
    coeff_shapes = [(nx + 1, FR, 128), fine, fine, fine, own_shape]
    mid_shapes = [(count + 1, MR, 128), mid, mid, mid, mid]
    coarse_shapes = [(half + 1, CR, 128), coarse, coarse, coarse]
    outs = call(
        functools.partial(second_kernel, nx, n_gy, min(unroll, 16)),
        coeff_shapes
        + [window, window, (2, 10, FR, 128)]
        + mid_shapes
        + coarse_shapes
        + [window, window, b1_shape, message_b, message_b, (WELLS, 128)],
        [fine_pad, fine, fine_pad, fine_pad, fine_pad, fine_pad, fine_pad, fine, (nx // 2, FR, 128)]
        + [mid_pad, mid, coarse_pad, coarse, mid, mid],
        [place] + owns + halos,
        1,
    )
    coeffs, (sto, d_one, bp) = outs[:5], outs[5:8]
    levels = list(outs[8:17])
    coeffs = list(coeffs)
    begun = outs[17:22]
    wells = None
    if use_list:
        lists = [outs[22], begun[3][-WELLS:], begun[4][-WELLS:]]
    else:
        wells = gathered_wells(well_rows, well_cells, well_counts, owners, well_start)
    scratch = [fine_pad, fine_pad, fine, (nx // 2, FR, 128)]
    scratch += [mid, mid_pad, mid_pad, mid, mid, coarse, coarse_pad, coarse_pad]
    change = None
    for kind in (1, 2, 3, 4):
        b_own, x_first, b1_own, up, down = begun
        below_b, above_b = exchange(up, down)
        if use_list and kind <= 2:
            lists += [below_b[-WELLS:]] if kind == 2 else [below_b[-WELLS:], above_b[-WELLS:]]
        x_own, b1_mid, up, down = call(
            functools.partial(middle_kernel, nx, unroll),
            [window, b1_shape, message_x, message_x],
            scratch,
            [b1_own, below_b, above_b] + levels + [b_own, x_first] + coeffs,
            0,
        )
        below, above = exchange(up, down)
        if use_list and kind == 1:
            lists += [below[-WELLS:], above[-WELLS:]]
        if kind == 2:
            wells = jnp.concatenate(lists, axis=1) if use_list else wells
            sources = well_sources(wells, nx, n_gy)
        extras = {1: lambda: [sto, d_one], 2: lambda: [sources[1]], 3: lambda: [sto, sources[0], change], 4: lambda: [lam_two, bp]}[
            kind
        ]()
        begin_shapes = [window, window, b1_shape, message_b, message_b]
        shapes = {
            1: begin_shapes + [window],
            2: begin_shapes + [(8, ROWS, 128)],
            3: begin_shapes + [(nx + 2, 40, 128)],
            4: [(8, ROWS, 128)],
        }[kind]
        outs = call(
            functools.partial(end_kernel, nx, n_gy, unroll, kind),
            shapes,
            scratch,
            [place, b1_mid, below, above] + levels + [below_b, above_b, b_own, x_own] + coeffs + extras,
            1,
        )
        if kind == 1:
            change = outs[5]
        elif kind == 2:
            final_change = outs[5]
        elif kind == 3:
            lam_two = outs[5]
        begun = outs[:5]
    return (outs[0], final_change)


def solution(mesh):
    return jax.shard_map(
        local,
        mesh=mesh,
        in_specs=(
            P("gx", "gy", None),
            P("gx", "gy", None),
            P("gx", "gy", None),
            P(None, "gx", "gy", None),
            P(("gx", "gy"), None),
            P(("gx", "gy")),
            P(("gx", "gy")),
            P(("gx", "gy"), None),
            P(("gx", "gy")),
        ),
        out_specs=(P("gx", "gy", None), P("gx", "gy", None)),
        check_vma=False,
    )
```

```python
import functools

import jax
import jax.numpy as jnp
from jax import lax
from jax.experimental import pallas as pl
from jax.experimental.pallas import tpu as pltpu
from jax.sharding import PartitionSpec as P

OMEGA = 0.8
KEEP = 0.2
VMEM_BYTES = 32 * 2**20
WELLS = 8

FR, MR, CR = 56, 64, 40
F_OWN, M_OWN = 12, 24
HALO_B, SKIP_B, HALO_X, SKIP_X = 4, 2, 3, 1
REACH_B, REACH_X = 14, 12
FIRST_ROWS = (7, 6, 3, 3, 3)
FIRST_AT = (0, 56, 104, 128, 152)
FIRST_WELLS, FIRST_MID, FIRST_SIZE = 176, 184, 248
OWN_WELLS, LATE_MID, LATE_BELOW, LATE_ABOVE = 1024, 256, 320, 384
ROWS = 32


def ds(start, size):
    return pl.ds(start, size)


def lanes(shape):
    return lax.broadcasted_iota(jnp.int32, shape, 1)


def loop(count, body, unroll):
    if unroll >= count:
        for index in range(count):
            body(index)
        return

    def step(index, carry):
        body(index)
        return carry

    lax.fori_loop(0, count, step, 0, unroll=unroll)


def neighbours(src, kx, ky, kz, x, start, size, shift):
    rows = ds(start, size)
    center = src[x + 1, rows, :]
    total = kx[x, rows, :] * src[x, rows, :] + kx[x + 1, rows, :] * src[x + 2, rows, :]
    total = total + ky[x, rows, :] * src[x + 1, ds(start + 1, size), :]
    total = total + ky[x, ds(start - 1, size), :] * src[x + 1, ds(start - 1, size), :]
    face = kz[x, rows, :]
    total = total + face * pltpu.roll(center, 128 - shift, 1) + pltpu.roll(face * center, shift, 1)
    return center, total


def sweep(src, dst, coeffs, b, start, size, count, shift, unroll):
    kx, ky, kz, w = coeffs
    rows = ds(start, size)

    def body(x):
        center, total = neighbours(src, kx, ky, kz, x, start, size, shift)
        dst[x + 1, rows, :] = KEEP * center + w[x, rows, :] * (b[x, rows, :] + total)

    loop(count, body, unroll)


def scaled(dst, w, b, start, size, count, unroll):
    rows = ds(start, size)

    def body(x):
        dst[x + 1, rows, :] = w[x, rows, :] * b[x, rows, :]

    loop(count, body, unroll)


def zero_ends(buf, count):
    buf[0] = jnp.zeros(buf.shape[1:], jnp.float32)
    buf[count + 1] = jnp.zeros(buf.shape[1:], jnp.float32)


def seam(buf, count, start, size, fill):
    rows = ds(start, size)
    odd = lanes((size, 128)) % 2 == 1
    buf[0, rows, :] = jnp.where(odd, pltpu.roll(buf[count, rows, :], 1, 1), fill)
    buf[count + 1, rows, :] = jnp.where(odd, fill, pltpu.roll(buf[1, rows, :], 127, 1))


def packed_sweep(src, dst, coeffs, b, start, size, count, shift, unroll):
    sweep(src, dst, coeffs, b, start, size, count, shift, unroll)
    seam(dst, count, start, size, 0.0)


def halve_packed(src, tmp, dst, count):
    for i in range(count // 2):
        tmp[i, ds(8, 48), :] = src[2 * i, ds(8, 48), :] + src[2 * i + 1, ds(8, 48), :]
    low = lanes((24, 128)) % 4 < 2
    for i in range(count // 2):
        both = tmp[i, pl.ds(8, 24, stride=2), :] + tmp[i, pl.ds(9, 24, stride=2), :]
        both = both + jnp.where(low, pltpu.roll(both, 126, 1), pltpu.roll(both, 2, 1))
        dst[i, ds(8, 24), :] = both * 0.125


def middle_solve(own, below, above, reach, mid, coarse, bufs, nx):
    m_b, m_a, m_c, m_res, m_tmp, c_b, c_a, c_c = bufs
    mkx, mky, mkz, mw, mdiag = mid
    count = nx // 4
    for i in range(count):
        m_b[i, ds(M_OWN - reach, reach), :] = below(i)
        m_b[i, ds(M_OWN, 16), :] = own(i)
        m_b[i, ds(M_OWN + 16, reach), :] = above(i)
    scaled(m_c, mw, m_b, 8, 48, count, count)
    seam(m_c, count, 8, 48, 0.0)
    packed_sweep(m_c, m_a, (mkx, mky, mkz, mw), m_b, 8, 48, count, 2, count)
    for i in range(count):
        center, total = neighbours(m_a, mkx, mky, mkz, i, 8, 48, 2)
        m_res[i, ds(8, 48), :] = m_b[i, ds(8, 48), :] + total - mdiag[i, ds(8, 48), :] * center
    halve_packed(m_res, m_tmp, c_b, count)
    half = count // 2
    scaled(c_a, coarse[3], c_b, 8, 24, half, half)
    seam(c_a, half, 8, 24, 0.0)
    packed_sweep(c_a, c_c, coarse, c_b, 8, 24, half, 4, half)
    packed_sweep(c_c, c_a, coarse, c_b, 8, 24, half, 4, half)
    packed_sweep(c_a, c_c, coarse, c_b, 8, 24, half, 4, half)
    for i in range(half):
        value = c_c[i + 1, ds(12, 16), :]
        m_tmp[i, pl.ds(16, 16, stride=2), :] = value
        m_tmp[i, pl.ds(17, 16, stride=2), :] = value
        for j in range(2):
            x = 2 * i + j + 1
            m_a[x, ds(16, 32), :] = m_a[x, ds(16, 32), :] + m_tmp[i, ds(16, 32), :]
    seam(m_a, count, 16, 32, 0.0)
    packed_sweep(m_a, m_c, (mkx, mky, mkz, mw), m_b, 16, 32, count, 2, count)
    packed_sweep(m_c, m_a, (mkx, mky, mkz, mw), m_b, 16, 32, count, 2, count)


def add_correction(x_buf, m_a, f_tmp, nx, unroll):
    count = nx // 4
    odd = lanes((24, 128)) % 2 == 1
    for i in range(count):
        value = m_a[i + 1, ds(20, 24), :]
        first = jnp.where(odd, pltpu.roll(value, 1, 1), value)
        second = jnp.where(odd, value, pltpu.roll(value, 127, 1))
        for part, slab in ((first, i), (second, i + count)):
            f_tmp[slab, pl.ds(4, 24, stride=2), :] = part
            f_tmp[slab, pl.ds(5, 24, stride=2), :] = part

    def body(i):
        value = f_tmp[i, ds(4, 48), :]
        for j in range(2):
            x = 2 * i + j + 1
            x_buf[x, ds(4, 48), :] = x_buf[x, ds(4, 48), :] + value

    loop(nx // 2, body, unroll)


def restricted(x_buf, coeffs, diag, b, f_tmp, outs, nx, unroll):
    kx, ky, kz, w = coeffs
    count = nx // 4

    def body(i):
        both = None
        for j in range(2):
            x = 2 * i + j
            center, total = neighbours(x_buf, kx, ky, kz, x, F_OWN, ROWS, 1)
            part = b[x, ds(F_OWN, ROWS), :] + total - diag[x] * center
            both = part if both is None else both + part
        f_tmp[i, ds(0, ROWS), :] = both

    loop(nx // 2, body, unroll)
    odd = lanes((16, 128)) % 2 == 1
    for i in range(count):
        first = f_tmp[i, pl.ds(0, 16, stride=2), :] + f_tmp[i, pl.ds(1, 16, stride=2), :]
        second = f_tmp[i + count, pl.ds(0, 16, stride=2), :] + f_tmp[i + count, pl.ds(1, 16, stride=2), :]
        value = 0.125 * jnp.where(
            odd, second + pltpu.roll(second, 1, 1), first + pltpu.roll(first, 127, 1)
        )
        for out in outs:
            out(i, value)


def gather_rows(buf, window, below, above, halo, skip, nx, pad, keep_low=None, keep_high=None):
    low, high = F_OWN - skip - halo, F_OWN + ROWS + skip
    for x in range(nx):
        buf[x + pad, ds(8, 40), :] = window[x]
        under, over = below[ds(x * halo, halo), :], above[ds(x * halo, halo), :]
        buf[x + pad, ds(low, halo), :] = under if keep_low is None else under * keep_low
        buf[x + pad, ds(high, halo), :] = over if keep_high is None else over * keep_high


def send_rows(up, down, buf, halo, skip, nx, pad):
    for x in range(nx):
        up[ds(x * halo, halo), :] = buf[x + pad, ds(F_OWN + ROWS - skip - halo, halo), :]
        down[ds(x * halo, halo), :] = buf[x + pad, ds(F_OWN + skip, halo), :]


def message_writers(ups, downs, b1_own, base, reach):
    def write(i, value):
        ups[ds(base + reach * i, reach), :] = value[16 - reach :]
        downs[ds(base + reach * i, reach), :] = value[:reach]
        b1_own[i] = value

    return [write]


def message_part(ref, base, reach):
    return lambda i: ref[ds(base + reach * i, reach), :]


def begin_solve(b_buf, x_a, x_b, coeffs, diag, f_tmp, b_out, x_out, b1_own, up, down, nx, unroll):
    scaled(x_a, coeffs[3], b_buf, 8, 40, nx, unroll)
    sweep(x_a, x_b, coeffs, b_buf, 8, 40, nx, 1, unroll)
    writers = message_writers(up, down, b1_own, nx * HALO_B, REACH_B)
    restricted(x_b, coeffs, diag, b_buf, f_tmp, writers, nx, unroll)
    for x in range(nx):
        b_out[x] = b_buf[x, ds(8, 40), :]
        x_out[x] = x_b[x + 1, ds(8, 40), :]
    send_rows(up, down, b_buf, HALO_B, SKIP_B, nx, 0)


def listed_wells(rows, counts, cells, owners, starts, masked):
    number, samples = rows.shape
    position = lanes((1, samples))
    lane = lanes((1, 128))
    listed = [jnp.full((1, 128), -1.0, jnp.float32)] + [jnp.zeros((1, 128), jnp.float32)] * 2
    masked[...] = jnp.zeros(masked.shape, jnp.float32)
    for i in range(number):
        masked[ds(i, 1), :] = jnp.where(position < counts[i], rows[ds(i, 1), :], 0.0)
        for j, ref in enumerate((owners, cells, starts)):
            listed[j] = jnp.where(lane == i, ref[i].astype(jnp.float32), listed[j])
    step = lax.broadcasted_iota(jnp.int32, (8, samples), 0)
    taken = jnp.where(lanes((8, samples)) // (samples // 2) == step, 1.0, 0.0)
    sums = lax.dot_general(
        taken, masked[...], (((1,), (1,)), ((), ())), precision=lax.Precision.HIGHEST, preferred_element_type=jnp.float32
    )
    return listed[0], listed[1], jnp.where(listed[2] <= 0.0, sums[0:1], 0.0), sums[1:2]


def first_kernel(use_list, *refs):
    if use_list:
        counts, cells, owners, starts, log, sto, per, bp, rows, own, late, up, down, tmp, masked = refs
    else:
        log, sto, per, bp, own, late, up, down, tmp = refs
    for ref, at in ((own, OWN_WELLS), (up, FIRST_WELLS), (down, FIRST_WELLS)):
        ref[ds(at, WELLS), :] = jnp.zeros((WELLS, 128), jnp.float32)
    if use_list:
        for j, value in enumerate(listed_wells(rows, counts, cells, owners, starts, masked)):
            for ref, at in ((own, OWN_WELLS), (up, FIRST_WELLS), (down, FIRST_WELLS)):
                ref[ds(at + j, 1), :] = value
    odd = lanes((16, 128)) % 2 == 1
    fields = (log, sto, per, bp.at[0], bp.at[1])
    for f, ref in enumerate(fields):
        for x in range(8):
            out, at = (own, f * 256) if f < 4 else (late, 0)
            out[ds(at + x * 32, 32), :] = ref[x]
    for f, (number, at) in enumerate(zip(FIRST_ROWS, FIRST_AT)):
        for x in range(8):
            up[ds(at + x * number, number), :] = fields[f][x, ds(32 - number, number), :]
            down[ds(at + x * number, number), :] = fields[f][x, ds(0, number), :]
    for i in range(4):
        tmp[0, i] = log[2 * i] + log[2 * i + 1]
        tmp[1, i] = sto[2 * i] + sto[2 * i + 1]
    for i in range(4):
        first, second = (
            tmp[f, i, pl.ds(0, 16, stride=2), :] + tmp[f, i, pl.ds(1, 16, stride=2), :] for f in range(2)
        )
        value = 0.125 * jnp.where(
            odd, second + pltpu.roll(second, 1, 1), first + pltpu.roll(first, 127, 1)
        )
        late[ds(LATE_MID + 16 * i, 16), :] = value
        up[ds(FIRST_MID + 16 * i, 16), :] = value
        down[ds(FIRST_MID + 16 * i, 16), :] = value


def faces(e, kx, ky, kz, count, size, shift, factor, unroll):
    top = lanes((size, 128)) >= 128 - shift

    def body(x):
        kx[x] = factor * e[x] * e[x + 1]
        center = e[x + 1]
        kz[x] = jnp.where(top, 0.0, factor * center * pltpu.roll(center, 128 - shift, 1))
        for start, number in ((0, size - 8), (size - 8, 7)):
            ky[x, ds(start, number), :] = factor * e[x + 1, ds(start, number), :] * e[x + 1, ds(start + 1, number), :]
        ky[x, ds(size - 1, 1), :] = jnp.zeros((1, 128), jnp.float32)

    loop(count, body, unroll)
    kx[count] = factor * e[count] * e[count + 1]


def diagonal(sto, kx, ky, kz, x, start, size, shift):
    rows = ds(start, size)
    face = kz[x, rows, :]
    total = sto + kx[x, rows, :] + kx[x + 1, rows, :] + ky[x, rows, :] + ky[x, ds(start - 1, size), :]
    return total + face + pltpu.roll(face, shift, 1)


def inside(size, own_start, own_size, first, last):
    row = lax.broadcasted_iota(jnp.int32, (size, 128), 0)
    return jnp.logical_and(
        jnp.logical_or(row >= own_start, jnp.logical_not(first)),
        jnp.logical_or(row < own_start + own_size, jnp.logical_not(last)),
    )


def blank(number):
    return jnp.zeros((number, 128), jnp.float32)


def place_rows(buf, slab, own, at, halo, f, x, keep_low, keep_high):
    number, start = FIRST_ROWS[f], FIRST_AT[f] + x * FIRST_ROWS[f]
    under, over = halo[ds(start, number), :], halo[ds(FIRST_MID + start, number), :]
    if f >= 2:
        under, over = under * keep_low, over * keep_high
    buf[slab, ds(F_OWN, ROWS), :] = own[ds(at, ROWS), :]
    buf[slab, ds(F_OWN - number, number), :] = under
    buf[slab, ds(F_OWN + ROWS, number), :] = over
    buf[slab, ds(0, F_OWN - number), :] = blank(F_OWN - number)
    buf[slab, ds(F_OWN + ROWS + number, F_OWN - number), :] = blank(F_OWN - number)


def tile_of(index, gx, tiles):
    half = tiles // 2
    k, other = index % half, index // half
    return ((gx // 2 + half - k) % half) * 2 + (gx % 2 + other) % 2


def change_terms(x, kx, ky, kz, per, bp):
    rows, plus, minus = ds(8, 40), ds(9, 40), ds(7, 40)
    face = kz[x, rows, :]
    c, p = per[x + 1, rows, :], bp[x + 1, rows, :]
    total = kx[x, rows, :] * (c + per[x, rows, :]) * (p - bp[x, rows, :])
    total = total + kx[x + 1, rows, :] * (c + per[x + 2, rows, :]) * (p - bp[x + 2, rows, :])
    total = total + ky[x, minus, :] * (c + per[x + 1, minus, :]) * (p - bp[x + 1, minus, :])
    total = total + ky[x, rows, :] * (c + per[x + 1, plus, :]) * (p - bp[x + 1, plus, :])
    flux = face * (c + pltpu.roll(c, 127, 1)) * (p - pltpu.roll(p, 127, 1))
    return 0.5 * (total + flux - pltpu.roll(flux, 1, 1))


def second_kernel(nx, n_gy, unroll, *refs):
    tiles = nx // 8
    place = refs[0]
    owns, halos = refs[1 : 1 + tiles], refs[1 + tiles : 1 + 2 * tiles]
    kx, ky, kz, w, diag, sto_out, per, bp0 = refs[1 + 2 * tiles : 9 + 2 * tiles]
    b_out, x_out, b1_own, up, down, wells = refs[9 + 2 * tiles : 15 + 2 * tiles]
    e, sto, x_a, x_b, b_buf, f_tmp = refs[15 + 2 * tiles :]
    gx, gy = place[0], place[1]
    first, last = gy == 0, gy == n_gy - 1
    for buf in (e, per, bp0, x_a, x_b):
        zero_ends(buf, nx)
    keep_low = jnp.where(first, 0.0, 1.0)
    keep_high = jnp.where(last, 0.0, 1.0)
    for index in range(tiles):
        own, halo = owns[index], halos[index]
        base = tile_of(index, gx, tiles) * 8

        for x in range(8):
            for f, buf in enumerate((e, sto, per, bp0)):
                slab = base + x + (0 if f == 1 else 1)
                place_rows(buf, slab, own, f * 256 + x * 32, halo, f, x, keep_low, keep_high)
    fine_inside = inside(FR, F_OWN, ROWS, first, last)

    def exps(x):
        e[x + 1] = jnp.where(fine_inside, jnp.exp(0.5 * e[x + 1]), 1.0)

    loop(nx, exps, unroll)
    e[0] = jnp.ones((FR, 128), jnp.float32)
    e[nx + 1] = jnp.ones((FR, 128), jnp.float32)
    faces(e, kx, ky, kz, nx, FR, 1, 1.0, unroll)
    win_inside = inside(48, F_OWN - 4, ROWS, first, last)

    def diagonals(x):
        value = diagonal(sto[x, ds(4, 48), :], kx, ky, kz, x, 4, 48, 1)
        w[x, ds(4, 48), :] = jnp.where(win_inside, OMEGA / value, 0.0)
        w[x, ds(0, 4), :] = blank(4)
        w[x, ds(52, 4), :] = blank(4)
        diag[x] = value[8:40]
        sto_out[x] = sto[x, ds(8, 40), :]

    loop(nx, diagonals, unroll)

    def changes(x):
        b_buf[x, ds(8, 40), :] = -change_terms(x, kx, ky, kz, per, bp0)

    loop(nx, changes, unroll)
    lane = lanes((WELLS, 128))
    listed = 128 // tiles
    for refs_of, at, out in ((owns, OWN_WELLS, wells), (halos, FIRST_WELLS, up), (halos, FIRST_MID + FIRST_WELLS, down)):
        value = refs_of[0][ds(at, WELLS), :]
        for index in range(1, tiles):
            moved = pltpu.roll(refs_of[index][ds(at, WELLS), :], index * listed, 1)
            value = jnp.where(lane >= index * listed, moved, value)
        out[ds(out.shape[0] - WELLS, WELLS), :] = value
    begin_solve(b_buf, x_a, x_b, (kx, ky, kz, w), diag, f_tmp, b_out, x_out, b1_own, up, down, nx, unroll)


def third_kernel(nx, n_gy, unroll, *refs):
    tiles = nx // 8
    half = tiles // 2
    place = refs[0]
    lates, halos = refs[1 : 1 + tiles], refs[1 + tiles : 1 + 2 * tiles]
    kx, ky, kz, per, bp0 = refs[1 + 2 * tiles : 6 + 2 * tiles]
    d_one, bp_out, mkx, mky, mkz, mw, mdiag, ckx, cky, ckz, cw = refs[6 + 2 * tiles : 17 + 2 * tiles]
    bp1, e_mid, s_mid, e_co, s_co, m_tmp, m_tmp2 = refs[17 + 2 * tiles :]
    gx, gy = place[0], place[1]
    first, last = gy == 0, gy == n_gy - 1
    keep_low = jnp.where(first, 0.0, 1.0)
    keep_high = jnp.where(last, 0.0, 1.0)
    zero_ends(bp1, nx)
    for index in range(tiles):
        base = tile_of(index, gx, tiles) * 8 + 1
        for x in range(8):
            place_rows(bp1, base + x, lates[index], x * 32, halos[index], 4, x, keep_low, keep_high)

    def changes(x):
        d_one[x] = change_terms(x, kx, ky, kz, per, bp1)

    loop(nx, changes, unroll)
    for x in range(10):
        bp_out[0, x] = bp0[gx * 8 + x]
        bp_out[1, x] = bp1[gx * 8 + x]

    count = nx // 4
    odd = lanes((16, 128)) % 2 == 1
    for index in range(tiles):
        late = lates[index]
        tile = tile_of(index, gx, tiles)
        upper = tile >= half
        base = jnp.where(upper, tile - half, tile) * 4
        mask = odd == upper
        for i in range(4):
            for start, at in ((8, LATE_BELOW), (24, LATE_MID), (40, LATE_ABOVE)):
                value = late[ds(at + 16 * i, 16), :]
                left, right = pltpu.roll(value, 127, 1), pltpu.roll(value, 1, 1)
                log_part, sto_part = jnp.where(odd, right, value), jnp.where(odd, value, left)
                rows = ds(start, 16)
                e_mid[base + i + 1, rows, :] = jnp.where(mask, log_part, e_mid[base + i + 1, rows, :])
                s_mid[base + i, rows, :] = jnp.where(mask, sto_part, s_mid[base + i, rows, :])
    for i in range(count):
        m_tmp2[i] = e_mid[i + 1]
    halve_packed(m_tmp2, m_tmp, e_co.at[pl.ds(1, count // 2)], count)
    halve_packed(s_mid, m_tmp, s_co, count)
    levels = (
        (e_mid, s_mid, mkx, mky, mkz, mw, mdiag, count, MR, M_OWN, 16, 2, 0.25),
        (e_co, s_co, ckx, cky, ckz, cw, None, count // 2, CR, 16, 8, 4, 0.0625),
    )
    for e_l, s_l, kx_l, ky_l, kz_l, w_l, diag_l, number, size, own_start, own_size, shift, factor in levels:
        ok = inside(size, own_start, own_size, first, last)
        row = lax.broadcasted_iota(jnp.int32, (size, 128), 0)
        ok = jnp.logical_and(ok, jnp.logical_and(row >= 8, row < size - 8))
        for i in range(number):
            e_l[i + 1] = jnp.where(ok, jnp.exp(0.5 * e_l[i + 1]), 1.0)
        seam(e_l, number, 0, size, 1.0)
        faces(e_l, kx_l, ky_l, kz_l, number, size, shift, factor, number)
        rows = ds(8, size - 16)
        edge = jnp.zeros((8, 128), jnp.float32)
        for i in range(number):
            value = diagonal(s_l[i, rows, :], kx_l, ky_l, kz_l, i, 8, size - 16, shift)
            w_l[i, rows, :] = jnp.where(ok[8 : size - 8], OMEGA / value, 0.0)
            w_l[i, ds(0, 8), :] = edge
            w_l[i, ds(size - 8, 8), :] = edge
            if diag_l is not None:
                diag_l[i, rows, :] = value
                diag_l[i, ds(0, 8), :] = edge
                diag_l[i, ds(size - 8, 8), :] = edge


def forward(below, above, up, down):
    up[ds(up.shape[0] - WELLS, WELLS), :] = below[ds(below.shape[0] - WELLS, WELLS), :]
    down[ds(down.shape[0] - WELLS, WELLS), :] = above[ds(above.shape[0] - WELLS, WELLS), :]


def middle_kernel(nx, unroll, *refs):
    b1_own, below, above, mkx, mky, mkz, mw, mdiag, ckx, cky, ckz, cw = refs[:12]
    b_in, x_in, kx, ky, kz, w, diag, x_out, b1_out, up, down = refs[12:23]
    x_a, x_b, b_buf, f_tmp = refs[23:27]
    bufs = refs[27:]
    coeffs = (kx, ky, kz, w)
    zero_ends(x_a, nx)
    zero_ends(x_b, nx)
    base = nx * HALO_B
    forward(below, above, up, down)
    middle_solve(
        lambda i: b1_own[i],
        message_part(below, base, REACH_B),
        message_part(above, base, REACH_B),
        REACH_B,
        (mkx, mky, mkz, mw, mdiag),
        (ckx, cky, ckz, cw),
        bufs,
        nx,
    )
    gather_rows(b_buf, b_in, below, above, HALO_B, SKIP_B, nx, 0)
    for start in (0, 40):
        scaled(x_a, w, b_buf, start, 16, nx, unroll)
    for x in range(nx):
        x_b[x + 1, ds(8, 40), :] = x_in[x]
    for start in (4, 44):
        sweep(x_a, x_b, coeffs, b_buf, start, 8, nx, 1, unroll)
    add_correction(x_b, bufs[1], f_tmp, nx, unroll)
    sweep(x_b, x_a, coeffs, b_buf, 8, 40, nx, 1, unroll)
    sweep(x_a, x_b, coeffs, b_buf, 8, 40, nx, 1, unroll)
    sweep(x_b, x_a, coeffs, b_buf, 8, 40, nx, 1, unroll)
    sweep(x_a, x_b, coeffs, b_buf, 8, 40, nx, 1, unroll)
    base = nx * HALO_X
    restricted(x_b, coeffs, diag, b_buf, f_tmp, message_writers(up, down, b1_out, base, REACH_X), nx, unroll)
    for x in range(nx):
        x_out[x] = x_b[x + 1, ds(8, 40), :]
    send_rows(up, down, x_b, HALO_X, SKIP_X, nx, 1)


def end_kernel(nx, n_gy, unroll, kind, *refs):
    place = refs[0]
    b1_in, below, above, mkx, mky, mkz, mw, mdiag, ckx, cky, ckz, cw = refs[1:13]
    below_b, above_b, b_in, x_in, kx, ky, kz, w, diag = refs[13:22]
    extra = {1: 2, 2: 1, 3: 3, 4: 2}[kind]
    extras, rest = refs[22 : 22 + extra], refs[22 + extra :]
    outs = {1: 6, 2: 6, 3: 6, 4: 1}[kind]
    outs, scratch = rest[:outs], rest[outs:]
    x_a, x_b, b_buf, f_tmp = scratch[:4]
    bufs = scratch[4:]
    coeffs = (kx, ky, kz, w)
    gx, gy = place[0], place[1]
    keep_low = jnp.where(gy == 0, 0.0, 1.0)
    keep_high = jnp.where(gy == n_gy - 1, 0.0, 1.0)
    zero_ends(x_a, nx)
    zero_ends(x_b, nx)
    base = nx * HALO_X
    if kind < 4:
        forward(below, above, outs[3], outs[4])
    middle_solve(
        lambda i: b1_in[i],
        message_part(below, base, REACH_X),
        message_part(above, base, REACH_X),
        REACH_X,
        (mkx, mky, mkz, mw, mdiag),
        (ckx, cky, ckz, cw),
        bufs,
        nx,
    )
    gather_rows(b_buf, b_in, below_b, above_b, HALO_B, SKIP_B, nx, 0)
    gather_rows(x_a, x_in, below, above, HALO_X, SKIP_X, nx, 1, keep_low, keep_high)
    add_correction(x_a, bufs[1], f_tmp, nx, unroll)
    sweep(x_a, x_b, coeffs, b_buf, 8, 40, nx, 1, unroll)
    sweep(x_b, x_a, coeffs, b_buf, 8, 40, nx, 1, unroll)
    rows = ds(8, 40)
    if kind < 4:
        b_out, x_out, b1_own, up, down, kept = outs

        def body(x):
            value = x_a[x + 1, rows, :]
            if kind == 1:
                sto, d_one = extras
                b_buf[x, rows, :] = sto[x] * value - d_one[x]
            elif kind == 2:
                b_buf[x, rows, :] = extras[0][x] * value
            else:
                sto, source, change = extras
                b_buf[x, rows, :] = sto[x] * value + source[x] * change[x]
            if kind == 1:
                kept[x] = value
            elif kind == 3:
                kept[x + 1] = value

        loop(nx, body, unroll)
        if kind == 2:
            for x in range(8):
                kept[x] = x_a[gx * 8 + x + 1, ds(F_OWN, ROWS), :]
        if kind == 3:
            zero_ends(kept, nx)
        begin_solve(b_buf, x_a, x_b, coeffs, diag, f_tmp, b_out, x_out, b1_own, up, down, nx, unroll)
    else:
        lam_two, bp = extras
        own, plus, minus = ds(F_OWN, ROWS), ds(F_OWN + 1, ROWS), ds(F_OWN - 1, ROWS)
        for x in range(8):
            at = gx * 8 + x
            kl, kr, kp, km, face = kx[at, own, :], kx[at + 1, own, :], ky[at, own, :], ky[at, minus, :], kz[at, own, :]
            total = None
            for t, (lam, shift) in enumerate(((x_a, 0), (lam_two, 8))):
                low, mid, high = (ds(F_OWN - shift + step, ROWS) for step in (-1, 0, 1))
                p, v = bp[t, x + 1, own, :], lam[at + 1, mid, :]
                part = kl * (p - bp[t, x, own, :]) * (v - lam[at, mid, :])
                part = part + kr * (p - bp[t, x + 2, own, :]) * (v - lam[at + 2, mid, :])
                part = part + km * (p - bp[t, x + 1, minus, :]) * (v - lam[at + 1, low, :])
                part = part + kp * (p - bp[t, x + 1, plus, :]) * (v - lam[at + 1, high, :])
                flux = face * (p - pltpu.roll(p, 127, 1)) * (v - pltpu.roll(v, 127, 1))
                part = part + flux + pltpu.roll(flux, 1, 1)
                total = part if total is None else total + part
            outs[0][x] = -0.5 * total


def call(body, outs, scratch, args, scalars, limit=VMEM_BYTES):
    f32 = jnp.float32
    staged = [i for i, arg in enumerate(args) if i >= scalars and arg.ndim == 1]
    held_at = len(args) + len(outs)

    def kernel(*refs):
        refs = list(refs)
        if staged:
            semaphores = refs[-1]
            copies = []
            for j, i in enumerate(staged):
                copies.append(pltpu.make_async_copy(refs[i], refs[held_at + j], semaphores.at[j]))
                copies[-1].start()
            for j, i in enumerate(staged):
                copies[j].wait()
                refs[i] = refs[held_at + j]
            refs = refs[:-1]
        body(*refs[:held_at], *refs[held_at + len(staged) :])

    return pl.pallas_call(
        kernel,
        out_shape=[jax.ShapeDtypeStruct(shape, f32) for shape in outs],
        in_specs=[pl.BlockSpec(memory_space=pltpu.SMEM)] * scalars
        + [pl.BlockSpec(memory_space=pltpu.VMEM)] * (len(args) - scalars),
        out_specs=[pl.BlockSpec(memory_space=pltpu.VMEM)] * len(outs),
        scratch_shapes=[pltpu.SMEM(args[i].shape, args[i].dtype) for i in staged]
        + [pltpu.VMEM(shape, f32) for shape in scratch]
        + ([pltpu.SemaphoreType.DMA((len(staged),))] if staged else []),
        compiler_params=pltpu.CompilerParams(vmem_limit_bytes=limit),
    )(*args)


def cycle(count, step):
    return [(i, (i + step) % count) for i in range(count)]


def same_core(array, tiles):
    half = tiles // 2
    parts = []
    for k in range(1, half):
        perm = [(2 * a + c, 2 * ((a + k) % half) + c) for a in range(half) for c in range(2)]
        parts.append(lax.ppermute(array, "gx", perm))
    return parts


def other_core(array, tiles):
    return lax.ppermute(array, "gx", [(i, i ^ 1) for i in range(tiles)])


def all_parts(array, swapped, same, tiles):
    return [array] + list(same) + [swapped] + [other_core(part, tiles) for part in same]


def gathered_wells(rows, cells, counts, owners, starts):
    listed, samples = rows.shape
    position = jnp.arange(samples, dtype=jnp.int32)
    counted = jnp.where(position[None, :] < counts[:, None], rows, 0.0)
    per_step = counted.reshape(listed, 2, samples // 2).sum(axis=2)
    weights = jnp.where(jnp.arange(2, dtype=jnp.int32)[None, :] >= starts[:, None], per_step, 0.0)
    places = jnp.stack([owners, cells], axis=0).astype(jnp.float32)
    return lax.all_gather(jnp.concatenate([places, weights.T], axis=0), ("gx", "gy"), axis=1, tiled=True)


def well_sources(wells, nx, n_gy):
    owner, cell, weights = wells[0].astype(jnp.int32), wells[1].astype(jnp.int32), wells[2:4]
    x = (owner // n_gy) * 8 + cell // (32 * 128)
    y = (owner % n_gy - lax.axis_index("gy")) * 32 + (cell // 128) % 32 + 4
    spot = jnp.where(jnp.logical_and(owner >= 0, jnp.logical_and(y >= 0, y < 40)), x * 40 + y, -1)
    z = cell % 128
    total = spot.shape[0]
    chunk = 1024 if total % 1024 == 0 else total

    def part(spot, z, weights):
        left = (spot[None, :] == jnp.arange(nx * 40, dtype=jnp.int32)[:, None]).astype(jnp.float32)
        here = z[:, None] == jnp.arange(128, dtype=jnp.int32)[None, :]
        right = jnp.concatenate([jnp.where(here, weights[t][:, None], 0.0) for t in range(2)], axis=1)
        return jnp.dot(left, right, precision=lax.Precision.HIGHEST)

    if total == chunk:
        source = part(spot, z, weights)
    else:

        def body(i, acc):
            cut = lambda a: lax.dynamic_slice_in_dim(a, i * chunk, chunk, axis=-1)
            return acc + part(cut(spot), cut(z), cut(weights))

        source = lax.fori_loop(0, total // chunk, body, jnp.zeros((nx * 40, 256), jnp.float32))
    return [source[:, t * 128 : (t + 1) * 128].reshape(nx, 40, 128) for t in range(2)]


def local(log_perm, perturb, storage, base_press, well_rows, well_cells, well_counts, well_owner, well_start):
    tiles, n_gy = lax.axis_size("gx"), lax.axis_size("gy")
    nx = 8 * tiles
    count, half = nx // 4, nx // 8
    unroll = 32
    up_perm, down_perm = cycle(n_gy, 1), cycle(n_gy, -1)

    def exchange(up, down):
        return lax.ppermute(up, "gy", up_perm), lax.ppermute(down, "gy", down_perm)

    place = jnp.stack([lax.axis_index("gx"), lax.axis_index("gy")]).astype(jnp.int32)
    listed, samples = well_rows.shape
    owners = well_owner.reshape(listed)
    use_list = n_gy == 8 and tiles * listed == 128
    own, late, up, down = call(
        functools.partial(first_kernel, use_list),
        [(OWN_WELLS + WELLS, 128), (LATE_BELOW, 128), (FIRST_SIZE, 128), (FIRST_SIZE, 128)],
        [(2, 4, 32, 128)] + ([(128, samples)] if use_list else []),
        ([well_counts, well_cells, owners, well_start] if use_list else [])
        + [log_perm, storage, perturb, base_press]
        + ([well_rows] if use_list else []),
        4 if use_list else 0,
        60 * 2**20,
    )
    below, above = exchange(up, down)
    own_same, own_swapped = same_core(own, tiles), other_core(own, tiles)
    halo = jnp.concatenate([below[:FIRST_MID], above[:FIRST_MID]], axis=0)
    halo_same, halo_swapped = same_core(halo, tiles), other_core(halo, tiles)
    late = jnp.concatenate([late, below[FIRST_MID:], above[FIRST_MID:]], axis=0)
    late_same, late_swapped = same_core(late, tiles), other_core(late, tiles)
    own_same, halo_same = lax.optimization_barrier((own_same, halo_same))
    owns = all_parts(own, own_swapped, own_same, tiles)
    halos = all_parts(halo, halo_swapped, halo_same, tiles)

    fine, fine_pad, mid, mid_pad = (nx, FR, 128), (nx + 2, FR, 128), (count, MR, 128), (count + 2, MR, 128)
    coarse, coarse_pad = (half, CR, 128), (half + 2, CR, 128)
    own_shape, window = (nx, ROWS, 128), (nx, 40, 128)
    b1_shape = (count, 16, 128)
    message_b = (nx * HALO_B + count * REACH_B + WELLS, 128)
    message_x = (nx * HALO_X + count * REACH_X + WELLS, 128)
    coeff_shapes = [(nx + 1, FR, 128), fine, fine, fine, own_shape]
    mid_shapes = [(count + 1, MR, 128), mid, mid, mid, mid]
    coarse_shapes = [(half + 1, CR, 128), coarse, coarse, coarse]
    outs = call(
        functools.partial(second_kernel, nx, n_gy, unroll),
        coeff_shapes
        + [window, fine_pad, fine_pad]
        + [window, window, b1_shape, message_b, message_b, (WELLS, 128)],
        [fine_pad, fine, fine_pad, fine_pad, fine, (nx // 2, FR, 128)],
        [place] + owns + halos,
        1,
    )
    coeffs, sto, begun = list(outs[:5]), outs[5], outs[8:13]
    own_wells = outs[13]
    late_same, _ = lax.optimization_barrier((late_same, begun))
    lates, begun = lax.optimization_barrier((all_parts(late, late_swapped, late_same, tiles), begun))
    later = call(
        functools.partial(third_kernel, nx, n_gy, unroll),
        [window, (2, 10, FR, 128)] + mid_shapes + coarse_shapes,
        [fine_pad, mid_pad, mid, coarse_pad, coarse, mid, mid],
        [place] + lates + halos + list(outs[:3]) + list(outs[6:8]),
        1,
    )
    d_one, bp, levels = later[0], later[1], list(later[2:])
    wells = None
    if use_list:
        lists = [own_wells, begun[3][-WELLS:], begun[4][-WELLS:]]
    else:
        wells = gathered_wells(well_rows, well_cells, well_counts, owners, well_start)
    scratch = [fine_pad, fine_pad, fine, (nx // 2, FR, 128)]
    scratch += [mid, mid_pad, mid_pad, mid, mid, coarse, coarse_pad, coarse_pad]
    change = None
    for kind in (1, 2, 3, 4):
        b_own, x_first, b1_own, up, down = begun
        below_b, above_b = exchange(up, down)
        if use_list and kind <= 2:
            lists += [below_b[-WELLS:]] if kind == 2 else [below_b[-WELLS:], above_b[-WELLS:]]
        x_own, b1_mid, up, down = call(
            functools.partial(middle_kernel, nx, unroll),
            [window, b1_shape, message_x, message_x],
            scratch,
            [b1_own, below_b, above_b] + levels + [b_own, x_first] + coeffs,
            0,
        )
        below, above = exchange(up, down)
        if use_list and kind == 1:
            lists += [below[-WELLS:], above[-WELLS:]]
        if kind == 2:
            wells = jnp.concatenate(lists, axis=1) if use_list else wells
            sources = well_sources(wells, nx, n_gy)
        extras = {1: lambda: [sto, d_one], 2: lambda: [sources[1]], 3: lambda: [sto, sources[0], change], 4: lambda: [lam_two, bp]}[
            kind
        ]()
        begin_shapes = [window, window, b1_shape, message_b, message_b]
        shapes = {
            1: begin_shapes + [window],
            2: begin_shapes + [(8, ROWS, 128)],
            3: begin_shapes + [(nx + 2, 40, 128)],
            4: [(8, ROWS, 128)],
        }[kind]
        outs = call(
            functools.partial(end_kernel, nx, n_gy, unroll, kind),
            shapes,
            scratch,
            [place, b1_mid, below, above] + levels + [below_b, above_b, b_own, x_own] + coeffs + extras,
            1,
        )
        if kind == 1:
            change = outs[5]
        elif kind == 2:
            final_change = outs[5]
        elif kind == 3:
            lam_two = outs[5]
        begun = outs[:5]
    return (outs[0], final_change)


def solution(mesh):
    return jax.shard_map(
        local,
        mesh=mesh,
        in_specs=(
            P("gx", "gy", None),
            P("gx", "gy", None),
            P("gx", "gy", None),
            P(None, "gx", "gy", None),
            P(("gx", "gy"), None),
            P(("gx", "gy")),
            P(("gx", "gy")),
            P(("gx", "gy"), None),
            P(("gx", "gy")),
        ),
        out_specs=(P("gx", "gy", None), P("gx", "gy", None)),
        check_vma=False,
    )
```

```python
import functools

import jax
import jax.numpy as jnp
from jax import lax
from jax.experimental import pallas as pl
from jax.experimental.pallas import tpu as pltpu
from jax.sharding import PartitionSpec as P

OMEGA = 0.8
KEEP = 0.2
VMEM_BYTES = 32 * 2**20
WELLS = 8

FR, MR, CR = 56, 64, 40
F_OWN, M_OWN = 12, 24
HALO_B, SKIP_B, HALO_X, SKIP_X = 4, 2, 3, 1
REACH_B, REACH_X = 14, 12
FIRST_ROWS = (7, 6, 3, 3, 3)
FIRST_AT = (0, 56, 104, 128, 152)
FIRST_WELLS, FIRST_MID, FIRST_SIZE = 176, 184, 248
OWN_WELLS, LATE_MID, LATE_BELOW, LATE_ABOVE = 1024, 256, 320, 384
ROWS = 32


def ds(start, size):
    return pl.ds(start, size)


def lanes(shape):
    return lax.broadcasted_iota(jnp.int32, shape, 1)


def loop(count, body, unroll):
    if unroll >= count:
        for index in range(count):
            body(index)
        return

    def step(index, carry):
        body(index)
        return carry

    lax.fori_loop(0, count, step, 0, unroll=unroll)


def neighbours(src, kx, ky, kz, x, start, size, shift):
    rows = ds(start, size)
    center = src[x + 1, rows, :]
    total = kx[x, rows, :] * src[x, rows, :] + kx[x + 1, rows, :] * src[x + 2, rows, :]
    total = total + ky[x, rows, :] * src[x + 1, ds(start + 1, size), :]
    total = total + ky[x, ds(start - 1, size), :] * src[x + 1, ds(start - 1, size), :]
    face = kz[x, rows, :]
    total = total + face * pltpu.roll(center, 128 - shift, 1) + pltpu.roll(face * center, shift, 1)
    return center, total


def sweep(src, dst, coeffs, b, start, size, count, shift, unroll):
    kx, ky, kz, w = coeffs
    rows = ds(start, size)

    def body(x):
        center, total = neighbours(src, kx, ky, kz, x, start, size, shift)
        dst[x + 1, rows, :] = KEEP * center + w[x, rows, :] * (b[x, rows, :] + total)

    loop(count, body, unroll)


def scaled(dst, w, b, start, size, count, unroll):
    rows = ds(start, size)

    def body(x):
        dst[x + 1, rows, :] = w[x, rows, :] * b[x, rows, :]

    loop(count, body, unroll)


def zero_ends(buf, count):
    buf[0] = jnp.zeros(buf.shape[1:], jnp.float32)
    buf[count + 1] = jnp.zeros(buf.shape[1:], jnp.float32)


def seam(buf, count, start, size, fill):
    rows = ds(start, size)
    odd = lanes((size, 128)) % 2 == 1
    buf[0, rows, :] = jnp.where(odd, pltpu.roll(buf[count, rows, :], 1, 1), fill)
    buf[count + 1, rows, :] = jnp.where(odd, fill, pltpu.roll(buf[1, rows, :], 127, 1))


def packed_sweep(src, dst, coeffs, b, start, size, count, shift, unroll):
    sweep(src, dst, coeffs, b, start, size, count, shift, unroll)
    seam(dst, count, start, size, 0.0)


def halve_packed(src, tmp, dst, count):
    for i in range(count // 2):
        tmp[i, ds(8, 48), :] = src[2 * i, ds(8, 48), :] + src[2 * i + 1, ds(8, 48), :]
    low = lanes((24, 128)) % 4 < 2
    for i in range(count // 2):
        both = tmp[i, pl.ds(8, 24, stride=2), :] + tmp[i, pl.ds(9, 24, stride=2), :]
        both = both + jnp.where(low, pltpu.roll(both, 126, 1), pltpu.roll(both, 2, 1))
        dst[i, ds(8, 24), :] = both * 0.125


def middle_solve(own, below, above, reach, mid, coarse, bufs, nx):
    m_b, m_a, m_c, m_res, m_tmp, c_b, c_a, c_c = bufs
    mkx, mky, mkz, mw, mdiag = mid
    count = nx // 4
    for i in range(count):
        m_b[i, ds(M_OWN - reach, reach), :] = below(i)
        m_b[i, ds(M_OWN, 16), :] = own(i)
        m_b[i, ds(M_OWN + 16, reach), :] = above(i)
    scaled(m_c, mw, m_b, 8, 48, count, count)
    seam(m_c, count, 8, 48, 0.0)
    packed_sweep(m_c, m_a, (mkx, mky, mkz, mw), m_b, 8, 48, count, 2, count)
    for i in range(count):
        center, total = neighbours(m_a, mkx, mky, mkz, i, 8, 48, 2)
        m_res[i, ds(8, 48), :] = m_b[i, ds(8, 48), :] + total - mdiag[i, ds(8, 48), :] * center
    halve_packed(m_res, m_tmp, c_b, count)
    half = count // 2
    scaled(c_a, coarse[3], c_b, 8, 24, half, half)
    seam(c_a, half, 8, 24, 0.0)
    packed_sweep(c_a, c_c, coarse, c_b, 8, 24, half, 4, half)
    packed_sweep(c_c, c_a, coarse, c_b, 8, 24, half, 4, half)
    packed_sweep(c_a, c_c, coarse, c_b, 8, 24, half, 4, half)
    for i in range(half):
        value = c_c[i + 1, ds(12, 16), :]
        m_tmp[i, pl.ds(16, 16, stride=2), :] = value
        m_tmp[i, pl.ds(17, 16, stride=2), :] = value
        for j in range(2):
            x = 2 * i + j + 1
            m_a[x, ds(16, 32), :] = m_a[x, ds(16, 32), :] + m_tmp[i, ds(16, 32), :]
    seam(m_a, count, 16, 32, 0.0)
    packed_sweep(m_a, m_c, (mkx, mky, mkz, mw), m_b, 16, 32, count, 2, count)
    packed_sweep(m_c, m_a, (mkx, mky, mkz, mw), m_b, 16, 32, count, 2, count)


def add_correction(x_buf, m_a, f_tmp, nx, unroll):
    count = nx // 4
    odd = lanes((24, 128)) % 2 == 1
    for i in range(count):
        value = m_a[i + 1, ds(20, 24), :]
        first = jnp.where(odd, pltpu.roll(value, 1, 1), value)
        second = jnp.where(odd, value, pltpu.roll(value, 127, 1))
        for part, slab in ((first, i), (second, i + count)):
            f_tmp[slab, pl.ds(4, 24, stride=2), :] = part
            f_tmp[slab, pl.ds(5, 24, stride=2), :] = part

    def body(i):
        value = f_tmp[i, ds(4, 48), :]
        for j in range(2):
            x = 2 * i + j + 1
            x_buf[x, ds(4, 48), :] = x_buf[x, ds(4, 48), :] + value

    loop(nx // 2, body, unroll)


def restricted(x_buf, coeffs, diag, b, f_tmp, outs, nx, unroll):
    kx, ky, kz, w = coeffs
    count = nx // 4

    def body(i):
        both = None
        for j in range(2):
            x = 2 * i + j
            center, total = neighbours(x_buf, kx, ky, kz, x, F_OWN, ROWS, 1)
            part = b[x, ds(F_OWN, ROWS), :] + total - diag[x] * center
            both = part if both is None else both + part
        f_tmp[i, ds(0, ROWS), :] = both

    loop(nx // 2, body, unroll)
    odd = lanes((16, 128)) % 2 == 1
    for i in range(count):
        first = f_tmp[i, pl.ds(0, 16, stride=2), :] + f_tmp[i, pl.ds(1, 16, stride=2), :]
        second = f_tmp[i + count, pl.ds(0, 16, stride=2), :] + f_tmp[i + count, pl.ds(1, 16, stride=2), :]
        value = 0.125 * jnp.where(
            odd, second + pltpu.roll(second, 1, 1), first + pltpu.roll(first, 127, 1)
        )
        for out in outs:
            out(i, value)


def gather_rows(buf, window, below, above, halo, skip, nx, pad, keep_low=None, keep_high=None):
    low, high = F_OWN - skip - halo, F_OWN + ROWS + skip
    for x in range(nx):
        buf[x + pad, ds(8, 40), :] = window[x]
        under, over = below[ds(x * halo, halo), :], above[ds(x * halo, halo), :]
        buf[x + pad, ds(low, halo), :] = under if keep_low is None else under * keep_low
        buf[x + pad, ds(high, halo), :] = over if keep_high is None else over * keep_high


def send_rows(up, down, buf, halo, skip, nx, pad):
    for x in range(nx):
        up[ds(x * halo, halo), :] = buf[x + pad, ds(F_OWN + ROWS - skip - halo, halo), :]
        down[ds(x * halo, halo), :] = buf[x + pad, ds(F_OWN + skip, halo), :]


def message_writers(ups, downs, b1_own, base, reach):
    def write(i, value):
        ups[ds(base + reach * i, reach), :] = value[16 - reach :]
        downs[ds(base + reach * i, reach), :] = value[:reach]
        b1_own[i] = value

    return [write]


def message_part(ref, base, reach):
    return lambda i: ref[ds(base + reach * i, reach), :]


def begin_solve(b_buf, x_a, x_b, coeffs, diag, f_tmp, b_out, x_out, b1_own, up, down, nx, unroll):
    scaled(x_a, coeffs[3], b_buf, 8, 40, nx, unroll)
    sweep(x_a, x_b, coeffs, b_buf, 8, 40, nx, 1, unroll)
    writers = message_writers(up, down, b1_own, nx * HALO_B, REACH_B)
    restricted(x_b, coeffs, diag, b_buf, f_tmp, writers, nx, unroll)
    for x in range(nx):
        b_out[x] = b_buf[x, ds(8, 40), :]
        x_out[x] = x_b[x + 1, ds(8, 40), :]
    send_rows(up, down, b_buf, HALO_B, SKIP_B, nx, 0)


def listed_wells(rows, counts, cells, owners, starts, masked):
    number, samples = rows.shape
    position = lanes((1, samples))
    lane = lanes((1, 128))
    listed = [jnp.full((1, 128), -1.0, jnp.float32)] + [jnp.zeros((1, 128), jnp.float32)] * 2
    masked[...] = jnp.zeros(masked.shape, jnp.float32)
    for i in range(number):
        masked[ds(i, 1), :] = jnp.where(position < counts[i], rows[ds(i, 1), :], 0.0)
        for j, ref in enumerate((owners, cells, starts)):
            listed[j] = jnp.where(lane == i, ref[i].astype(jnp.float32), listed[j])
    step = lax.broadcasted_iota(jnp.int32, (8, samples), 0)
    taken = jnp.where(lanes((8, samples)) // (samples // 2) == step, 1.0, 0.0)
    sums = lax.dot_general(
        taken, masked[...], (((1,), (1,)), ((), ())), precision=lax.Precision.HIGHEST, preferred_element_type=jnp.float32
    )
    return listed[0], listed[1], jnp.where(listed[2] <= 0.0, sums[0:1], 0.0), sums[1:2]


def first_kernel(use_list, *refs):
    if use_list:
        counts, cells, owners, starts, log, sto, per, bp, rows, own, late, up, down, tmp, masked = refs
    else:
        log, sto, per, bp, own, late, up, down, tmp = refs
    for ref, at in ((own, OWN_WELLS), (up, FIRST_WELLS), (down, FIRST_WELLS)):
        ref[ds(at, WELLS), :] = jnp.zeros((WELLS, 128), jnp.float32)
    if use_list:
        for j, value in enumerate(listed_wells(rows, counts, cells, owners, starts, masked)):
            for ref, at in ((own, OWN_WELLS), (up, FIRST_WELLS), (down, FIRST_WELLS)):
                ref[ds(at + j, 1), :] = value
    odd = lanes((16, 128)) % 2 == 1
    fields = (log, sto, per, bp.at[0], bp.at[1])
    for f, ref in enumerate(fields):
        for x in range(8):
            out, at = (own, f * 256) if f < 4 else (late, 0)
            out[ds(at + x * 32, 32), :] = ref[x]
    for f, (number, at) in enumerate(zip(FIRST_ROWS, FIRST_AT)):
        for x in range(8):
            up[ds(at + x * number, number), :] = fields[f][x, ds(32 - number, number), :]
            down[ds(at + x * number, number), :] = fields[f][x, ds(0, number), :]
    for i in range(4):
        tmp[0, i] = log[2 * i] + log[2 * i + 1]
        tmp[1, i] = sto[2 * i] + sto[2 * i + 1]
    for i in range(4):
        first, second = (
            tmp[f, i, pl.ds(0, 16, stride=2), :] + tmp[f, i, pl.ds(1, 16, stride=2), :] for f in range(2)
        )
        value = 0.125 * jnp.where(
            odd, second + pltpu.roll(second, 1, 1), first + pltpu.roll(first, 127, 1)
        )
        late[ds(LATE_MID + 16 * i, 16), :] = value
        up[ds(FIRST_MID + 16 * i, 16), :] = value
        down[ds(FIRST_MID + 16 * i, 16), :] = value


def faces(e, kx, ky, kz, count, size, shift, factor, unroll):
    top = lanes((size, 128)) >= 128 - shift

    def body(x):
        kx[x] = factor * e[x] * e[x + 1]
        center = e[x + 1]
        kz[x] = jnp.where(top, 0.0, factor * center * pltpu.roll(center, 128 - shift, 1))
        for start, number in ((0, size - 8), (size - 8, 7)):
            ky[x, ds(start, number), :] = factor * e[x + 1, ds(start, number), :] * e[x + 1, ds(start + 1, number), :]
        ky[x, ds(size - 1, 1), :] = jnp.zeros((1, 128), jnp.float32)

    loop(count, body, unroll)
    kx[count] = factor * e[count] * e[count + 1]


def diagonal(sto, kx, ky, kz, x, start, size, shift):
    rows = ds(start, size)
    face = kz[x, rows, :]
    total = sto + kx[x, rows, :] + kx[x + 1, rows, :] + ky[x, rows, :] + ky[x, ds(start - 1, size), :]
    return total + face + pltpu.roll(face, shift, 1)


def inside(size, own_start, own_size, first, last):
    row = lax.broadcasted_iota(jnp.int32, (size, 128), 0)
    return jnp.logical_and(
        jnp.logical_or(row >= own_start, jnp.logical_not(first)),
        jnp.logical_or(row < own_start + own_size, jnp.logical_not(last)),
    )


def blank(number):
    return jnp.zeros((number, 128), jnp.float32)


def place_rows(buf, slab, own, at, halo, f, x, keep_low, keep_high):
    number, start = FIRST_ROWS[f], FIRST_AT[f] + x * FIRST_ROWS[f]
    under, over = halo[ds(start, number), :], halo[ds(FIRST_MID + start, number), :]
    if f >= 2:
        under, over = under * keep_low, over * keep_high
    buf[slab, ds(F_OWN, ROWS), :] = own[ds(at, ROWS), :]
    buf[slab, ds(F_OWN - number, number), :] = under
    buf[slab, ds(F_OWN + ROWS, number), :] = over
    buf[slab, ds(0, F_OWN - number), :] = blank(F_OWN - number)
    buf[slab, ds(F_OWN + ROWS + number, F_OWN - number), :] = blank(F_OWN - number)


def tile_of(index, gx, tiles):
    half = tiles // 2
    k, other = index % half, index // half
    return ((gx // 2 + half - k) % half) * 2 + (gx % 2 + other) % 2


def change_terms(x, kx, ky, kz, per, bp):
    rows, plus, minus = ds(8, 40), ds(9, 40), ds(7, 40)
    face = kz[x, rows, :]
    c, p = per[x + 1, rows, :], bp[x + 1, rows, :]
    total = kx[x, rows, :] * (c + per[x, rows, :]) * (p - bp[x, rows, :])
    total = total + kx[x + 1, rows, :] * (c + per[x + 2, rows, :]) * (p - bp[x + 2, rows, :])
    total = total + ky[x, minus, :] * (c + per[x + 1, minus, :]) * (p - bp[x + 1, minus, :])
    total = total + ky[x, rows, :] * (c + per[x + 1, plus, :]) * (p - bp[x + 1, plus, :])
    flux = face * (c + pltpu.roll(c, 127, 1)) * (p - pltpu.roll(p, 127, 1))
    return 0.5 * (total + flux - pltpu.roll(flux, 1, 1))


def second_kernel(nx, n_gy, unroll, *refs):
    tiles = nx // 8
    place = refs[0]
    owns, halos = refs[1 : 1 + tiles], refs[1 + tiles : 1 + 2 * tiles]
    kx, ky, kz, w, diag, sto_out, per, bp0 = refs[1 + 2 * tiles : 9 + 2 * tiles]
    b_out, x_out, b1_own, up, down, wells = refs[9 + 2 * tiles : 15 + 2 * tiles]
    e, sto, x_a, x_b, b_buf, f_tmp = refs[15 + 2 * tiles :]
    gx, gy = place[0], place[1]
    first, last = gy == 0, gy == n_gy - 1
    for buf in (e, per, bp0, x_a, x_b):
        zero_ends(buf, nx)
    keep_low = jnp.where(first, 0.0, 1.0)
    keep_high = jnp.where(last, 0.0, 1.0)
    for index in range(tiles):
        own, halo = owns[index], halos[index]
        base = tile_of(index, gx, tiles) * 8

        for x in range(8):
            for f, buf in enumerate((e, sto, per, bp0)):
                slab = base + x + (0 if f == 1 else 1)
                place_rows(buf, slab, own, f * 256 + x * 32, halo, f, x, keep_low, keep_high)
    fine_inside = inside(FR, F_OWN, ROWS, first, last)

    def exps(x):
        e[x + 1] = jnp.where(fine_inside, jnp.exp(0.5 * e[x + 1]), 1.0)

    loop(nx, exps, unroll)
    e[0] = jnp.ones((FR, 128), jnp.float32)
    e[nx + 1] = jnp.ones((FR, 128), jnp.float32)
    faces(e, kx, ky, kz, nx, FR, 1, 1.0, unroll)
    win_inside = inside(48, F_OWN - 4, ROWS, first, last)

    def diagonals(x):
        value = diagonal(sto[x, ds(4, 48), :], kx, ky, kz, x, 4, 48, 1)
        w[x, ds(4, 48), :] = jnp.where(win_inside, OMEGA / value, 0.0)
        w[x, ds(0, 4), :] = blank(4)
        w[x, ds(52, 4), :] = blank(4)
        diag[x] = value[8:40]
        sto_out[x] = sto[x, ds(8, 40), :]

    loop(nx, diagonals, unroll)

    def changes(x):
        b_buf[x, ds(8, 40), :] = -change_terms(x, kx, ky, kz, per, bp0)

    loop(nx, changes, unroll)
    lane = lanes((WELLS, 128))
    listed = 128 // tiles
    for refs_of, at, out in ((owns, OWN_WELLS, wells), (halos, FIRST_WELLS, up), (halos, FIRST_MID + FIRST_WELLS, down)):
        value = refs_of[0][ds(at, WELLS), :]
        for index in range(1, tiles):
            moved = pltpu.roll(refs_of[index][ds(at, WELLS), :], index * listed, 1)
            value = jnp.where(lane >= index * listed, moved, value)
        out[ds(out.shape[0] - WELLS, WELLS), :] = value
    begin_solve(b_buf, x_a, x_b, (kx, ky, kz, w), diag, f_tmp, b_out, x_out, b1_own, up, down, nx, unroll)


def third_kernel(nx, n_gy, unroll, *refs):
    tiles = nx // 8
    half = tiles // 2
    place = refs[0]
    lates, halos = refs[1 : 1 + tiles], refs[1 + tiles : 1 + 2 * tiles]
    kx, ky, kz, per, bp0 = refs[1 + 2 * tiles : 6 + 2 * tiles]
    d_one, bp_out, mkx, mky, mkz, mw, mdiag, ckx, cky, ckz, cw = refs[6 + 2 * tiles : 17 + 2 * tiles]
    bp1, e_mid, s_mid, e_co, s_co, m_tmp, m_tmp2 = refs[17 + 2 * tiles :]
    gx, gy = place[0], place[1]
    first, last = gy == 0, gy == n_gy - 1
    keep_low = jnp.where(first, 0.0, 1.0)
    keep_high = jnp.where(last, 0.0, 1.0)
    zero_ends(bp1, nx)
    for index in range(tiles):
        base = tile_of(index, gx, tiles) * 8 + 1
        for x in range(8):
            place_rows(bp1, base + x, lates[index], x * 32, halos[index], 4, x, keep_low, keep_high)

    def changes(x):
        d_one[x] = change_terms(x, kx, ky, kz, per, bp1)

    loop(nx, changes, unroll)
    for x in range(10):
        bp_out[0, x] = bp0[gx * 8 + x]
        bp_out[1, x] = bp1[gx * 8 + x]

    count = nx // 4
    odd = lanes((16, 128)) % 2 == 1
    for index in range(tiles):
        late = lates[index]
        tile = tile_of(index, gx, tiles)
        upper = tile >= half
        base = jnp.where(upper, tile - half, tile) * 4
        mask = odd == upper
        for i in range(4):
            for start, at in ((8, LATE_BELOW), (24, LATE_MID), (40, LATE_ABOVE)):
                value = late[ds(at + 16 * i, 16), :]
                left, right = pltpu.roll(value, 127, 1), pltpu.roll(value, 1, 1)
                log_part, sto_part = jnp.where(odd, right, value), jnp.where(odd, value, left)
                rows = ds(start, 16)
                e_mid[base + i + 1, rows, :] = jnp.where(mask, log_part, e_mid[base + i + 1, rows, :])
                s_mid[base + i, rows, :] = jnp.where(mask, sto_part, s_mid[base + i, rows, :])
    for i in range(count):
        m_tmp2[i] = e_mid[i + 1]
    halve_packed(m_tmp2, m_tmp, e_co.at[pl.ds(1, count // 2)], count)
    halve_packed(s_mid, m_tmp, s_co, count)
    levels = (
        (e_mid, s_mid, mkx, mky, mkz, mw, mdiag, count, MR, M_OWN, 16, 2, 0.25),
        (e_co, s_co, ckx, cky, ckz, cw, None, count // 2, CR, 16, 8, 4, 0.0625),
    )
    for e_l, s_l, kx_l, ky_l, kz_l, w_l, diag_l, number, size, own_start, own_size, shift, factor in levels:
        ok = inside(size, own_start, own_size, first, last)
        row = lax.broadcasted_iota(jnp.int32, (size, 128), 0)
        ok = jnp.logical_and(ok, jnp.logical_and(row >= 8, row < size - 8))
        for i in range(number):
            e_l[i + 1] = jnp.where(ok, jnp.exp(0.5 * e_l[i + 1]), 1.0)
        seam(e_l, number, 0, size, 1.0)
        faces(e_l, kx_l, ky_l, kz_l, number, size, shift, factor, number)
        rows = ds(8, size - 16)
        edge = jnp.zeros((8, 128), jnp.float32)
        for i in range(number):
            value = diagonal(s_l[i, rows, :], kx_l, ky_l, kz_l, i, 8, size - 16, shift)
            w_l[i, rows, :] = jnp.where(ok[8 : size - 8], OMEGA / value, 0.0)
            w_l[i, ds(0, 8), :] = edge
            w_l[i, ds(size - 8, 8), :] = edge
            if diag_l is not None:
                diag_l[i, rows, :] = value
                diag_l[i, ds(0, 8), :] = edge
                diag_l[i, ds(size - 8, 8), :] = edge


def forward(below, above, up, down):
    up[ds(up.shape[0] - WELLS, WELLS), :] = below[ds(below.shape[0] - WELLS, WELLS), :]
    down[ds(down.shape[0] - WELLS, WELLS), :] = above[ds(above.shape[0] - WELLS, WELLS), :]


def middle_kernel(nx, unroll, *refs):
    b1_own, below, above, mkx, mky, mkz, mw, mdiag, ckx, cky, ckz, cw = refs[:12]
    b_in, x_in, kx, ky, kz, w, diag, x_out, b1_out, up, down = refs[12:23]
    x_a, x_b, b_buf, f_tmp = refs[23:27]
    bufs = refs[27:]
    coeffs = (kx, ky, kz, w)
    zero_ends(x_a, nx)
    zero_ends(x_b, nx)
    base = nx * HALO_B
    forward(below, above, up, down)
    middle_solve(
        lambda i: b1_own[i],
        message_part(below, base, REACH_B),
        message_part(above, base, REACH_B),
        REACH_B,
        (mkx, mky, mkz, mw, mdiag),
        (ckx, cky, ckz, cw),
        bufs,
        nx,
    )
    gather_rows(b_buf, b_in, below, above, HALO_B, SKIP_B, nx, 0)
    for start in (0, 40):
        scaled(x_a, w, b_buf, start, 16, nx, unroll)
    for x in range(nx):
        x_b[x + 1, ds(8, 40), :] = x_in[x]
    for start in (4, 44):
        sweep(x_a, x_b, coeffs, b_buf, start, 8, nx, 1, unroll)
    add_correction(x_b, bufs[1], f_tmp, nx, unroll)
    sweep(x_b, x_a, coeffs, b_buf, 8, 40, nx, 1, unroll)
    sweep(x_a, x_b, coeffs, b_buf, 8, 40, nx, 1, unroll)
    sweep(x_b, x_a, coeffs, b_buf, 8, 40, nx, 1, unroll)
    sweep(x_a, x_b, coeffs, b_buf, 8, 40, nx, 1, unroll)
    base = nx * HALO_X
    restricted(x_b, coeffs, diag, b_buf, f_tmp, message_writers(up, down, b1_out, base, REACH_X), nx, unroll)
    for x in range(nx):
        x_out[x] = x_b[x + 1, ds(8, 40), :]
    send_rows(up, down, x_b, HALO_X, SKIP_X, nx, 1)


def end_kernel(nx, n_gy, unroll, kind, *refs):
    place = refs[0]
    b1_in, below, above, mkx, mky, mkz, mw, mdiag, ckx, cky, ckz, cw = refs[1:13]
    below_b, above_b, b_in, x_in, kx, ky, kz, w, diag = refs[13:22]
    extra = {1: 2, 2: 1, 3: 3, 4: 2}[kind]
    extras, rest = refs[22 : 22 + extra], refs[22 + extra :]
    outs = {1: 6, 2: 6, 3: 6, 4: 1}[kind]
    outs, scratch = rest[:outs], rest[outs:]
    x_a, x_b, b_buf, f_tmp = scratch[:4]
    bufs = scratch[4:]
    coeffs = (kx, ky, kz, w)
    gx, gy = place[0], place[1]
    keep_low = jnp.where(gy == 0, 0.0, 1.0)
    keep_high = jnp.where(gy == n_gy - 1, 0.0, 1.0)
    zero_ends(x_a, nx)
    zero_ends(x_b, nx)
    base = nx * HALO_X
    if kind < 4:
        forward(below, above, outs[3], outs[4])
    middle_solve(
        lambda i: b1_in[i],
        message_part(below, base, REACH_X),
        message_part(above, base, REACH_X),
        REACH_X,
        (mkx, mky, mkz, mw, mdiag),
        (ckx, cky, ckz, cw),
        bufs,
        nx,
    )
    gather_rows(b_buf, b_in, below_b, above_b, HALO_B, SKIP_B, nx, 0)
    gather_rows(x_a, x_in, below, above, HALO_X, SKIP_X, nx, 1, keep_low, keep_high)
    add_correction(x_a, bufs[1], f_tmp, nx, unroll)
    sweep(x_a, x_b, coeffs, b_buf, 8, 40, nx, 1, unroll)
    sweep(x_b, x_a, coeffs, b_buf, 8, 40, nx, 1, unroll)
    rows = ds(8, 40)
    if kind < 4:
        b_out, x_out, b1_own, up, down, kept = outs

        def body(x):
            value = x_a[x + 1, rows, :]
            if kind == 1:
                sto, d_one = extras
                b_buf[x, rows, :] = sto[x] * value - d_one[x]
            elif kind == 2:
                b_buf[x, rows, :] = extras[0][x] * value
            else:
                sto, source, change = extras
                b_buf[x, rows, :] = sto[x] * value + source[x] * change[x]
            if kind == 1:
                kept[x] = value
            elif kind == 3:
                kept[x + 1] = value

        loop(nx, body, unroll)
        if kind == 2:
            for x in range(8):
                kept[x] = x_a[gx * 8 + x + 1, ds(F_OWN, ROWS), :]
        if kind == 3:
            zero_ends(kept, nx)
        begin_solve(b_buf, x_a, x_b, coeffs, diag, f_tmp, b_out, x_out, b1_own, up, down, nx, unroll)
    else:
        lam_two, bp = extras
        own, plus, minus = ds(F_OWN, ROWS), ds(F_OWN + 1, ROWS), ds(F_OWN - 1, ROWS)
        for x in range(8):
            at = gx * 8 + x
            kl, kr, kp, km, face = kx[at, own, :], kx[at + 1, own, :], ky[at, own, :], ky[at, minus, :], kz[at, own, :]
            total = None
            for t, (lam, shift) in enumerate(((x_a, 0), (lam_two, 8))):
                low, mid, high = (ds(F_OWN - shift + step, ROWS) for step in (-1, 0, 1))
                p, v = bp[t, x + 1, own, :], lam[at + 1, mid, :]
                part = kl * (p - bp[t, x, own, :]) * (v - lam[at, mid, :])
                part = part + kr * (p - bp[t, x + 2, own, :]) * (v - lam[at + 2, mid, :])
                part = part + km * (p - bp[t, x + 1, minus, :]) * (v - lam[at + 1, low, :])
                part = part + kp * (p - bp[t, x + 1, plus, :]) * (v - lam[at + 1, high, :])
                flux = face * (p - pltpu.roll(p, 127, 1)) * (v - pltpu.roll(v, 127, 1))
                part = part + flux + pltpu.roll(flux, 1, 1)
                total = part if total is None else total + part
            outs[0][x] = -0.5 * total


def call(body, outs, scratch, args, scalars, limit=VMEM_BYTES):
    f32 = jnp.float32
    staged = [i for i, arg in enumerate(args) if i >= scalars and arg.ndim == 1]
    held_at = len(args) + len(outs)

    def kernel(*refs):
        refs = list(refs)
        if staged:
            semaphores = refs[-1]
            copies = []
            for j, i in enumerate(staged):
                copies.append(pltpu.make_async_copy(refs[i], refs[held_at + j], semaphores.at[j]))
                copies[-1].start()
            for j, i in enumerate(staged):
                copies[j].wait()
                refs[i] = refs[held_at + j]
            refs = refs[:-1]
        body(*refs[:held_at], *refs[held_at + len(staged) :])

    return pl.pallas_call(
        kernel,
        out_shape=[jax.ShapeDtypeStruct(shape, f32) for shape in outs],
        in_specs=[pl.BlockSpec(memory_space=pltpu.SMEM)] * scalars
        + [pl.BlockSpec(memory_space=pltpu.VMEM)] * (len(args) - scalars),
        out_specs=[pl.BlockSpec(memory_space=pltpu.VMEM)] * len(outs),
        scratch_shapes=[pltpu.SMEM(args[i].shape, args[i].dtype) for i in staged]
        + [pltpu.VMEM(shape, f32) for shape in scratch]
        + ([pltpu.SemaphoreType.DMA((len(staged),))] if staged else []),
        compiler_params=pltpu.CompilerParams(vmem_limit_bytes=limit),
    )(*args)


def cycle(count, step):
    return [(i, (i + step) % count) for i in range(count)]


def same_core(array, tiles):
    half = tiles // 2
    parts = []
    for k in range(1, half):
        perm = [(2 * a + c, 2 * ((a + k) % half) + c) for a in range(half) for c in range(2)]
        parts.append(lax.ppermute(array, "gx", perm))
    return parts


def other_core(array, tiles):
    return lax.ppermute(array, "gx", [(i, i ^ 1) for i in range(tiles)])


def all_parts(array, swapped, same, tiles):
    return [array] + list(same) + [swapped] + [other_core(part, tiles) for part in same]


def gathered_wells(rows, cells, counts, owners, starts):
    listed, samples = rows.shape
    position = jnp.arange(samples, dtype=jnp.int32)
    counted = jnp.where(position[None, :] < counts[:, None], rows, 0.0)
    per_step = counted.reshape(listed, 2, samples // 2).sum(axis=2)
    weights = jnp.where(jnp.arange(2, dtype=jnp.int32)[None, :] >= starts[:, None], per_step, 0.0)
    places = jnp.stack([owners, cells], axis=0).astype(jnp.float32)
    return lax.all_gather(jnp.concatenate([places, weights.T], axis=0), ("gx", "gy"), axis=1, tiled=True)


def well_sources(wells, nx, n_gy):
    owner, cell, weights = wells[0].astype(jnp.int32), wells[1].astype(jnp.int32), wells[2:4]
    x = (owner // n_gy) * 8 + cell // (32 * 128)
    y = (owner % n_gy - lax.axis_index("gy")) * 32 + (cell // 128) % 32 + 4
    spot = jnp.where(jnp.logical_and(owner >= 0, jnp.logical_and(y >= 0, y < 40)), x * 40 + y, -1)
    z = cell % 128
    total = spot.shape[0]
    chunk = 1024 if total % 1024 == 0 else total

    def part(spot, z, weights):
        left = (spot[None, :] == jnp.arange(nx * 40, dtype=jnp.int32)[:, None]).astype(jnp.float32)
        here = z[:, None] == jnp.arange(128, dtype=jnp.int32)[None, :]
        right = jnp.concatenate([jnp.where(here, weights[t][:, None], 0.0) for t in range(2)], axis=1)
        return jnp.dot(left, right, precision=lax.Precision.HIGHEST)

    if total == chunk:
        source = part(spot, z, weights)
    else:

        def body(i, acc):
            cut = lambda a: lax.dynamic_slice_in_dim(a, i * chunk, chunk, axis=-1)
            return acc + part(cut(spot), cut(z), cut(weights))

        source = lax.fori_loop(0, total // chunk, body, jnp.zeros((nx * 40, 256), jnp.float32))
    return [source[:, t * 128 : (t + 1) * 128].reshape(nx, 40, 128) for t in range(2)]


def local(log_perm, perturb, storage, base_press, well_rows, well_cells, well_counts, well_owner, well_start):
    tiles, n_gy = lax.axis_size("gx"), lax.axis_size("gy")
    nx = 8 * tiles
    count, half = nx // 4, nx // 8
    unroll = 32
    up_perm, down_perm = cycle(n_gy, 1), cycle(n_gy, -1)

    def exchange(up, down):
        return lax.ppermute(up, "gy", up_perm), lax.ppermute(down, "gy", down_perm)

    place = jnp.stack([lax.axis_index("gx"), lax.axis_index("gy")]).astype(jnp.int32)
    listed, samples = well_rows.shape
    owners = well_owner.reshape(listed)
    use_list = n_gy == 8 and tiles * listed == 128
    own, late, up, down = call(
        functools.partial(first_kernel, use_list),
        [(OWN_WELLS + WELLS, 128), (LATE_BELOW, 128), (FIRST_SIZE, 128), (FIRST_SIZE, 128)],
        [(2, 4, 32, 128)] + ([(128, samples)] if use_list else []),
        ([well_counts, well_cells, owners, well_start] if use_list else [])
        + [log_perm, storage, perturb, base_press]
        + ([well_rows] if use_list else []),
        4 if use_list else 0,
        60 * 2**20,
    )
    below, above = exchange(up, down)
    own_same, own_swapped = same_core(own, tiles), other_core(own, tiles)
    halo = jnp.concatenate([below[:FIRST_MID], above[:FIRST_MID]], axis=0)
    halo_same, halo_swapped = same_core(halo, tiles), other_core(halo, tiles)
    late = jnp.concatenate([late, below[FIRST_MID:], above[FIRST_MID:]], axis=0)
    late_same, late_swapped = same_core(late, tiles), other_core(late, tiles)
    own_same, halo_same = lax.optimization_barrier((own_same, halo_same))
    owns = all_parts(own, own_swapped, own_same, tiles)
    halos = all_parts(halo, halo_swapped, halo_same, tiles)

    fine, fine_pad, mid, mid_pad = (nx, FR, 128), (nx + 2, FR, 128), (count, MR, 128), (count + 2, MR, 128)
    coarse, coarse_pad = (half, CR, 128), (half + 2, CR, 128)
    own_shape, window = (nx, ROWS, 128), (nx, 40, 128)
    b1_shape = (count, 16, 128)
    message_b = (nx * HALO_B + count * REACH_B + WELLS, 128)
    message_x = (nx * HALO_X + count * REACH_X + WELLS, 128)
    coeff_shapes = [(nx + 1, FR, 128), fine, fine, fine, own_shape]
    mid_shapes = [(count + 1, MR, 128), mid, mid, mid, mid]
    coarse_shapes = [(half + 1, CR, 128), coarse, coarse, coarse]
    outs = call(
        functools.partial(second_kernel, nx, n_gy, unroll),
        coeff_shapes
        + [window, fine_pad, fine_pad]
        + [window, window, b1_shape, message_b, message_b, (WELLS, 128)],
        [fine_pad, fine, fine_pad, fine_pad, fine, (nx // 2, FR, 128)],
        [place] + owns + halos,
        1,
    )
    coeffs, sto, begun = list(outs[:5]), outs[5], outs[8:13]
    own_wells = outs[13]
    late_same, _ = lax.optimization_barrier((late_same, begun))
    begun = list(begun)
    lates, begun[4] = lax.optimization_barrier((all_parts(late, late_swapped, late_same, tiles), begun[4]))
    later = call(
        functools.partial(third_kernel, nx, n_gy, unroll),
        [window, (2, 10, FR, 128)] + mid_shapes + coarse_shapes,
        [fine_pad, mid_pad, mid, coarse_pad, coarse, mid, mid],
        [place] + lates + halos + list(outs[:3]) + list(outs[6:8]),
        1,
    )
    d_one, bp, levels = later[0], later[1], list(later[2:])
    wells = None
    if use_list:
        lists = [own_wells, begun[3][-WELLS:], begun[4][-WELLS:]]
    else:
        wells = gathered_wells(well_rows, well_cells, well_counts, owners, well_start)
    scratch = [fine_pad, fine_pad, fine, (nx // 2, FR, 128)]
    scratch += [mid, mid_pad, mid_pad, mid, mid, coarse, coarse_pad, coarse_pad]
    change = None
    for kind in (1, 2, 3, 4):
        b_own, x_first, b1_own, up, down = begun
        below_b, above_b = exchange(up, down)
        if use_list and kind <= 2:
            lists += [below_b[-WELLS:]] if kind == 2 else [below_b[-WELLS:], above_b[-WELLS:]]
        x_own, b1_mid, up, down = call(
            functools.partial(middle_kernel, nx, unroll),
            [window, b1_shape, message_x, message_x],
            scratch,
            [b1_own, below_b, above_b] + levels + [b_own, x_first] + coeffs,
            0,
        )
        below, above = exchange(up, down)
        if use_list and kind == 1:
            lists += [below[-WELLS:], above[-WELLS:]]
        if kind == 2:
            wells = jnp.concatenate(lists, axis=1) if use_list else wells
            sources = well_sources(wells, nx, n_gy)
        extras = {1: lambda: [sto, d_one], 2: lambda: [sources[1]], 3: lambda: [sto, sources[0], change], 4: lambda: [lam_two, bp]}[
            kind
        ]()
        begin_shapes = [window, window, b1_shape, message_b, message_b]
        shapes = {
            1: begin_shapes + [window],
            2: begin_shapes + [(8, ROWS, 128)],
            3: begin_shapes + [(nx + 2, 40, 128)],
            4: [(8, ROWS, 128)],
        }[kind]
        outs = call(
            functools.partial(end_kernel, nx, n_gy, unroll, kind),
            shapes,
            scratch,
            [place, b1_mid, below, above] + levels + [below_b, above_b, b_own, x_own] + coeffs + extras,
            1,
        )
        if kind == 1:
            change = outs[5]
        elif kind == 2:
            final_change = outs[5]
        elif kind == 3:
            lam_two = outs[5]
        begun = outs[:5]
    return (outs[0], final_change)


def solution(mesh):
    return jax.shard_map(
        local,
        mesh=mesh,
        in_specs=(
            P("gx", "gy", None),
            P("gx", "gy", None),
            P("gx", "gy", None),
            P(None, "gx", "gy", None),
            P(("gx", "gy"), None),
            P(("gx", "gy")),
            P(("gx", "gy")),
            P(("gx", "gy"), None),
            P(("gx", "gy")),
        ),
        out_specs=(P("gx", "gy", None), P("gx", "gy", None)),
        check_vma=False,
    )
```
